512 devices in a mesh: rows: 16 (over x, y_lo, core), cols: 32 (over y_hi, z).
Axes of the slice: x: 4, y: 4 (y_hi: 2, y_lo: 2; y = y_hi * 2 + y_lo), z: 16, core: 2. Of those that a mesh axis runs over, the one named last changes fastest.
Arguments:
- features: bfloat16 [16384, 512], P(('rows', 'cols')), may hold values from -0.59765625 to 0.59765625
- positions: float32 [3, 16384], P(None, ('rows', 'cols')), may hold values from 0 to 1, as said below
- cell_lengths: float32 [3], replicated, may hold values from 30 to 60
- block_lists: int32 [512, 8], P(('rows', 'cols')), may hold values from 0 to 511, as said below
- image_offsets: int32 [3, 512, 8], P(None, ('rows', 'cols')), may hold values from -1 to 1
- block_valid: int32 [512, 8], P(('rows', 'cols')), may hold values from 0 to 1, as said below
- norm_gain: float32 [512], replicated, may hold values from 0.1 to 1.9
- w_qkv: bfloat16 [512, 1536], replicated, may hold values from -1 to 1
- w_out: bfloat16 [512, 512], replicated, may hold values from -0.25 to 0.25
- rbf_weight: float32 [16, 64], replicated, may hold values from -5 to 5
- rbf_offset: float32 [64], replicated, may hold values from -4 to 4
- pair_weight: float32 [64, 16], replicated, may hold values from -30 to 30
- cosine_scale: float32 [16], replicated, may hold values from -80 to 80, as said below
Outputs:
- updated: bfloat16 [16384, 512], P(('rows', 'cols'))
The draws below stay inside these ranges and needn't reach their ends.
Inputs may be any that keep to these rules, and one draw needn't show every extreme that they name: `block_lists`: block b lies at grid row b // 32 and column b % 32. Every entry names a block whose row and column each differ from b's by at most one, counted around the grid; the first entry is b itself and the entries of a block differ. `block_valid`: the first entry of every block is 1 and a block's ones come before its zeros; some block has all 8 entries 1. `positions`: atoms of block b have their first coordinate within [r, r + 1] / 16 and their second within [c, c + 1] / 32, with r = b // 32 and c = b % 32. `cosine_scale`: every magnitude is 0.3 or more.
All inputs are finite; a program needn't handle non-finite values.
Results may differ from the reference program's by a relative error of at most 0.012.
The reference program's roundings to bfloat16 on the way (of `normed`, `packed`, `local_out`, `global_out` and `combined`) count: a program that leaves them out, or rounds other values in their place, can miss the bound.
Values may be sent and summed in bfloat16 or wider, within the bound.
A program may use at most 64 MiB of HBM per device.

```python
import math
import jax
import jax.numpy as jnp
import numpy as np
from jax import lax

D = 512
H = 16
PAIR = 64
NRBF = 16
LIST = 8
ATOM_DEV = 32
GROWS = 16
GCOLS = 32
BLOCKS = 512
ATOMS = 16384


neighbour_moves = np.array([[-1, -1], [-1, 0], [-1, 1], [0, -1], [0, 1], [1, -1], [1, 0], [1, 1]], dtype=np.int32)


def draw_positions(key, part):
    fraction = jax.random.uniform(key, (3, ATOMS), jnp.float32)
    block_ids = jnp.arange(ATOMS, dtype=jnp.int32) // ATOM_DEV
    row_of = (block_ids // GCOLS).astype(jnp.float32)
    col_of = (block_ids % GCOLS).astype(jnp.float32)
    return jnp.stack([(row_of + fraction[0]) / GROWS, (col_of + fraction[1]) / GCOLS, fraction[2]])


def draw_block_lists(key, part):
    scores = jax.random.randint(key, (BLOCKS, 8), 0, 1 << 20) * 8 + jnp.arange(8, dtype=jnp.int32)[None, :]
    picked = jnp.argsort(scores, axis=1, stable=True)[:, :LIST - 1]
    moves = jnp.asarray(neighbour_moves)[picked]
    block_ids = jnp.arange(BLOCKS, dtype=jnp.int32)
    row_of = block_ids // GCOLS
    col_of = block_ids % GCOLS
    listed = (row_of[:, None] + moves[:, :, 0]) % GROWS * GCOLS + (col_of[:, None] + moves[:, :, 1]) % GCOLS
    return jnp.concatenate([block_ids[:, None], listed], axis=1).astype(jnp.int32)


def draw_block_valid(key, part):
    extra = jax.random.randint(key, (BLOCKS,), 2, LIST)
    extra = jnp.where(jnp.arange(BLOCKS) == 0, LIST - 1, extra)
    return (jnp.arange(LIST, dtype=jnp.int32)[None, :] <= extra[:, None]).astype(jnp.int32)


def draw_w_qkv(key, part):
    columns = jnp.arange(3 * D, dtype=jnp.int32)
    spread = jnp.where(columns < 2 * D, 2.3, 1.0).astype(jnp.float32) / math.sqrt(D)
    base = jnp.clip(jax.random.normal(jax.random.fold_in(key, 5), (D, 3 * D), jnp.float32), -4.0, 4.0)
    return jnp.clip(base * spread[None, :], -1.0, 1.0).astype(jnp.bfloat16)


def draw_pair_weight(key, part):
    base = jnp.clip(jax.random.normal(jax.random.fold_in(key, 1), (PAIR, H), jnp.float32), -4.0, 4.0) / math.sqrt(PAIR)
    upper = 3.0
    scales = jnp.exp(jax.random.uniform(jax.random.fold_in(key, 2), (H,), jnp.float32, math.log(0.5), math.log(upper)))
    return jnp.clip(base * scales[None, :], -30.0, 30.0)


def draw_cosine_scale(key, part):
    upper = 24.0
    magnitude = jnp.exp(jax.random.uniform(jax.random.fold_in(key, 3), (H,), jnp.float32, math.log(0.3), math.log(upper)))
    order = jax.random.permutation(jax.random.fold_in(key, 4), H)
    signs = jnp.where(order < H // 2, -1.0, 1.0).astype(jnp.float32)
    return magnitude * signs


def with_ends(values, stream_key, smallest, high):
    dims = values.shape
    place = [jax.random.randint(jax.random.fold_in(stream_key, axis), (), 0, dims[axis]) for axis in range(len(dims))]
    values = values.at[tuple(place)].set(smallest)
    longest = dims.index(max(dims))
    place[longest] = (place[longest] + 1) % dims[longest]
    return values.at[tuple(place)].set(high)


def shard_levels(rng, extent, shards, low, largest):
    loudness, own = 1.0, jax.random.fold_in(rng, 6)
    for axis_at, parts in shards:
        steps = jnp.exp(jax.random.uniform(jax.random.fold_in(own, axis_at), (parts,), jnp.float32, low / len(shards), largest / len(shards)))
        loudness = loudness * jnp.repeat(steps, extent[axis_at] // parts).reshape([-1 if axis == axis_at else 1 for axis in range(len(extent))])
    return loudness


def centred(rng, extent, scale, bound, shards=(), kind=jnp.bfloat16):
    loudness = shard_levels(rng, extent, shards, -0.22, 0.18) if shards else 1.0
    values = jax.random.normal(rng, extent, jnp.float32) * scale * loudness
    return jnp.minimum(jnp.maximum(values, -bound), bound).astype(kind)


def setup_inputs(seed: int = 0) -> dict:
    splits = jax.random.split(jax.random.key(seed), 14)
    features = centred(splits[0], (ATOMS, D), 0.1, 0.59765625, ((0, 512),))
    positions = draw_positions(jax.random.fold_in(splits[13], 71), 0)
    cell_lengths = jnp.clip(jnp.exp(jax.random.uniform(splits[2], (3,), jnp.float32, math.log(30.0), math.log(60.0))), 30.0, 60.0)
    block_lists = draw_block_lists(jax.random.fold_in(splits[13], 71), 0)
    image_offsets = with_ends(jax.random.randint(splits[4], (3, BLOCKS, LIST), -1, 2), jax.random.fold_in(splits[4], 1), -1, 1).astype(jnp.int32)
    block_valid = draw_block_valid(jax.random.fold_in(splits[13], 71), 0)
    norm_gain = jnp.clip(1.0 + 0.18 * jax.random.normal(splits[6], (D,), jnp.float32), 0.1, 1.9)
    w_qkv = draw_w_qkv(jax.random.fold_in(splits[13], 71), 0)
    w_out = centred(splits[8], (D, D), D ** -0.5, 0.25)
    rbf_weight = centred(splits[9], (NRBF, PAIR), 1.0, 5.0, (), jnp.float32)
    rbf_offset = centred(splits[10], (PAIR,), 1.0, 4.0, (), jnp.float32)
    pair_weight = draw_pair_weight(jax.random.fold_in(splits[13], 71), 0)
    cosine_scale = draw_cosine_scale(jax.random.fold_in(splits[13], 71), 0)
    return {"features": features, "positions": positions, "cell_lengths": cell_lengths, "block_lists": block_lists, "image_offsets": image_offsets, "block_valid": block_valid, "norm_gain": norm_gain, "w_qkv": w_qkv, "w_out": w_out, "rbf_weight": rbf_weight, "rbf_offset": rbf_offset, "pair_weight": pair_weight, "cosine_scale": cosine_scale}


rbf_step = 2.0
rbf_width = 2.0
two_pi = 2.0 * math.pi
highest = lax.Precision.HIGHEST

def rounded(value):
    return lax.optimization_barrier(value.astype(jnp.bfloat16))

def rms_rows(values, norm_gain):
    floats = values.astype(jnp.float32)
    spread = lax.optimization_barrier(jnp.mean(floats * floats, axis=-1, keepdims=True))
    return rounded(floats * lax.rsqrt(spread + 1e-06) * norm_gain)

def near_attention(query_rows, own_pos, keys, key_pos, shifts, live, cell_lengths, rbf_weight, rbf_offset, pair_weight):
    entries, block_len = (keys.shape[0], keys.shape[1])
    model_dim = query_rows.shape[1]
    head_count = pair_weight.shape[1]
    head_dim = model_dim // head_count
    key_coords = key_pos.transpose(1, 0, 2) + shifts.astype(jnp.float32)[:, :, None]
    key_coords = key_coords.reshape(3, entries * block_len)
    displace = (key_coords[:, None, :] - own_pos[:, :, None]) * cell_lengths[:, None, None]
    distance = jnp.sqrt(lax.optimization_barrier(jnp.sum(displace * displace, axis=0)) + 0.25)
    centers = jnp.arange(rbf_weight.shape[0], dtype=jnp.float32) * rbf_step
    radial = jnp.exp(-(distance[None] - centers[:, None, None]) ** 2 * (0.5 / rbf_width ** 2))
    radial = radial.reshape(rbf_weight.shape[0], -1)
    hidden = jax.nn.silu(jnp.dot(rbf_weight.T, radial, precision=highest) + rbf_offset[:, None])
    pair_bias = jnp.dot(pair_weight.T, hidden, precision=highest).reshape(head_count, query_rows.shape[0], entries * block_len)
    query_heads = query_rows.reshape(-1, head_count, head_dim).astype(jnp.float32)
    key_heads = keys[:, :, :model_dim].reshape(entries * block_len, head_count, head_dim).astype(jnp.float32)
    value_heads = keys[:, :, model_dim:].reshape(entries * block_len, head_count, head_dim).astype(jnp.float32)
    scores = jnp.einsum('ahd,khd->hak', query_heads, key_heads, precision=highest) * head_dim ** (-0.5) + pair_bias
    allowed = jnp.repeat(live > 0, block_len)
    scores = jnp.where(allowed[None, None, :], scores, -1e+30)
    row_max = lax.optimization_barrier(jnp.max(scores, axis=-1, keepdims=True))
    weights = jnp.exp(scores - row_max)
    row_sum = lax.optimization_barrier(jnp.sum(weights, axis=-1, keepdims=True))
    prob_bf = rounded(weights).astype(jnp.float32)
    attended = jnp.einsum('hak,khd->ahd', prob_bf, value_heads, precision=highest) / row_sum.transpose(1, 0, 2)
    return rounded(attended.reshape(-1, model_dim))

def reference(features, positions, cell_lengths, block_lists, image_offsets, block_valid, norm_gain, w_qkv, w_out, rbf_weight, rbf_offset, pair_weight, cosine_scale):
    model_dim = features.shape[1]
    head_count = pair_weight.shape[1]
    head_dim = model_dim // head_count
    normed = rms_rows(features, norm_gain)
    packed = rounded(jnp.dot(normed, w_qkv, preferred_element_type=jnp.float32))
    kv_blocks = packed[:, model_dim:].reshape(BLOCKS, ATOM_DEV, 2 * model_dim)
    query_blocks = packed[:, :model_dim].reshape(BLOCKS, ATOM_DEV, model_dim)
    pos_blocks = positions.reshape(3, BLOCKS, ATOM_DEV).transpose(1, 0, 2)
    shift_blocks = image_offsets.transpose(1, 0, 2)

    def one_block(inputs):
        query_rows, own_pos, listed, shifts, live = inputs
        return near_attention(query_rows, own_pos, kv_blocks[listed], pos_blocks[listed], shifts, live, cell_lengths, rbf_weight, rbf_offset, pair_weight)
    local_out = lax.map(one_block, (query_blocks, pos_blocks, block_lists, shift_blocks, block_valid)).reshape(ATOMS, model_dim)
    angles = two_pi * positions
    coord_feats = jnp.concatenate([jnp.cos(angles), jnp.sin(angles)], axis=0)
    heads_first = packed.reshape(ATOMS, 3, head_count, head_dim).transpose(1, 2, 0, 3)
    query_len = ATOM_DEV * GCOLS

    def one_head(inputs):
        query_all, key_all, value_all, strength = inputs
        key_f = key_all.astype(jnp.float32)
        value_f = value_all.astype(jnp.float32)

        def one_rows(block_in):
            query_rows, query_feats = block_in
            scores = jnp.dot(query_rows.astype(jnp.float32), key_f.T, precision=highest) * head_dim ** (-0.5)
            scores = scores + strength * jnp.dot(query_feats.T, coord_feats, precision=highest)
            row_max = lax.optimization_barrier(jnp.max(scores, axis=-1, keepdims=True))
            weights = jnp.exp(scores - row_max)
            row_sum = lax.optimization_barrier(jnp.sum(weights, axis=-1))
            prob_bf = rounded(weights).astype(jnp.float32)
            return rounded(jnp.dot(prob_bf, value_f, precision=highest) / row_sum[:, None])
        query_split = query_all.reshape(ATOMS // query_len, query_len, head_dim)
        feat_split = coord_feats.reshape(6, ATOMS // query_len, query_len).transpose(1, 0, 2)
        return lax.map(one_rows, (query_split, feat_split)).reshape(ATOMS, head_dim)
    global_heads = lax.map(one_head, (heads_first[0], heads_first[1], heads_first[2], cosine_scale))
    global_out = global_heads.transpose(1, 0, 2).reshape(ATOMS, model_dim)
    combined = rounded(local_out.astype(jnp.float32) + global_out.astype(jnp.float32))
    updated = features.astype(jnp.float32) + jnp.dot(combined, w_out, preferred_element_type=jnp.float32)
    return updated.astype(jnp.bfloat16)
```

```python
import functools
import math

import jax
import jax.numpy as jnp
from jax import lax
from jax.experimental import pallas as pl
from jax.experimental.pallas import tpu as pltpu
from jax.sharding import PartitionSpec as P

MESH = pl.DeviceIdType.MESH
F32 = jnp.float32
BF16 = jnp.bfloat16
LOG2E = math.log2(math.e)

ATOMS = 32
WIDTH = 512
HEADS = 16
HEAD = 32
GROUP = 512
KEYS = 256
ROWS = 16
COLS = 32
RING = 16
RIGHT = 8
LEFT = 7


def tdot(a, b):
    return lax.dot_general(a, b, (((0,), (0,)), ((), ())), preferred_element_type=F32)


def split(value):
    high = value.astype(BF16)
    return high, (value - high.astype(F32)).astype(BF16)


def kernel(
    features,
    positions,
    lengths,
    lists,
    offsets,
    valid,
    gain,
    w_qkv,
    w_out,
    rbf_weight,
    rbf_offset,
    pair_weight,
    strengths,
    out,
    near_kv,
    near_pos,
    pieces,
    gathered,
    kv,
    queries,
    scores,
    run_max,
    accum,
    dist,
    bias,
    returning,
    returned,
    own_q,
    pos_send,
    pos_recv,
    halo_send,
    halo_recv,
    swap_send,
    swap_recv,
    ring_send,
    ring_recv,
    pair_send,
    pair_recv,
    back_send,
    back_recv,
):
    row, col = lax.axis_index("rows"), lax.axis_index("cols")
    core = lax.rem(row, 2)
    x, y_lo = row // 4, lax.rem(row // 2, 2)
    y_hi, z = col // RING, lax.rem(col, RING)
    group = x * 4 + y_hi * 2 + y_lo

    def plane(step):
        other = lax.rem(group + step, HEADS)
        ox, oy = other // 4, lax.rem(other, 4)
        return other, (ox * 4 + lax.rem(oy, 2) * 2 + core, oy // 2 * RING + z)

    right = (row, y_hi * RING + lax.rem(z + 1, RING))
    left = (row, y_hi * RING + lax.rem(z + RING - 1, RING))
    sibling = (row + 1 - 2 * core, col)

    def beside(dr, dc):
        return (lax.rem(row + dr + ROWS, ROWS), lax.rem(col + dc + COLS, COLS))

    moves = [(dr, dc) for dr in (-1, 0, 1) for dc in (-1, 0, 1) if (dr, dc) != (0, 0)]

    def remote(src, dst, send, recv, device):
        return pltpu.make_async_remote_copy(
            src_ref=src, dst_ref=dst, send_sem=send, recv_sem=recv, device_id=device, device_id_type=MESH
        )

    barrier = pltpu.get_barrier_semaphore()

    def greet(device):
        pl.semaphore_signal(barrier, inc=1, device_id=device, device_id_type=MESH)

    def greet_plane(step, carry):
        greet(plane(step)[1])
        return carry

    lax.fori_loop(1, HEADS, greet_plane, 0)
    for move in moves:
        greet(beside(*move))
    for device in (right, left, sibling):
        greet(device)

    pos = positions[...]
    near_pos[4] = jnp.zeros((8, 128), F32)
    near_pos[4, 0:3, 0:ATOMS] = pos
    angles = (2.0 * math.pi) * pos
    waves = jnp.concatenate(
        [jnp.cos(angles), jnp.sin(angles), jnp.ones((1, ATOMS), F32), jnp.zeros((1, ATOMS), F32)], axis=0
    )
    wave_high = waves.astype(BF16).astype(F32)
    waves = jnp.concatenate([wave_high, waves - wave_high], axis=0).astype(BF16)
    place = lax.broadcasted_iota(jnp.int32, (16, 128), 0) + 96 == lax.broadcasted_iota(jnp.int32, (16, 128), 1)
    wave_lanes = tdot(waves, jnp.where(place, 1.0, 0.0).astype(BF16))[:, 96:128]

    floats = features[...].astype(F32)
    spread = jnp.mean(floats * floats, axis=-1, keepdims=True)
    normed = (floats * lax.rsqrt(spread + 1e-06) * gain[...]).astype(BF16)
    packed = jnp.dot(normed, w_qkv[...], preferred_element_type=F32)
    for head in range(HEADS):
        lo = head * HEAD
        pieces[head] = jnp.concatenate(
            [
                packed[:, lo : lo + HEAD],
                packed[:, WIDTH + lo : WIDTH + lo + HEAD],
                packed[:, 2 * WIDTH + lo : 2 * WIDTH + lo + HEAD],
                wave_lanes,
            ],
            axis=1,
        ).astype(BF16)
    own_q[...] = packed[:, :WIDTH].astype(BF16)
    near_kv[4] = packed[:, WIDTH:].astype(BF16)

    pl.semaphore_wait(barrier, HEADS - 1 + len(moves) + 3)

    def pos_copy(k):
        dr, dc = moves[k]
        return remote(
            near_pos.at[4],
            near_pos.at[(1 - dr) * 3 + (1 - dc)],
            pos_send.at[k],
            pos_recv.at[k],
            beside(dr, dc),
        )

    def swap_copy(step):
        other, device = plane(step)
        return remote(
            pieces.at[other],
            gathered.at[pl.ds(pl.multiple_of(group * ATOMS, ATOMS), ATOMS)],
            swap_send.at[step],
            swap_recv.at[step],
            device,
        )

    def start_swap(step, carry):
        swap_copy(step).start()
        return carry

    lax.fori_loop(1, HEADS, start_swap, 0)
    for k in range(len(moves)):
        pos_copy(k).start()
    gathered[pl.ds(pl.multiple_of(group * ATOMS, ATOMS), ATOMS), :] = pieces[group]

    halo_copies = [
        remote(near_kv.at[4], near_kv.at[3], halo_send.at[0], halo_recv.at[0], beside(0, 1)),
        remote(near_kv.at[4], near_kv.at[5], halo_send.at[1], halo_recv.at[1], beside(0, -1)),
        remote(near_kv.at[pl.ds(3, 3)], near_kv.at[pl.ds(0, 3)], halo_send.at[2], halo_recv.at[2], beside(1, 0)),
        remote(near_kv.at[pl.ds(3, 3)], near_kv.at[pl.ds(6, 3)], halo_send.at[3], halo_recv.at[3], beside(-1, 0)),
    ]
    halo_copies[0].start()
    halo_copies[1].start()

    for k in range(len(moves)):
        pos_copy(k).wait_recv()
    slots = []
    for e in range(8):
        block = lists[0, e]
        dr = lax.rem(block // COLS - row + 1 + ROWS, ROWS)
        dc = lax.rem(lax.rem(block, COLS) - col + 1 + COLS, COLS)
        slots.append(jnp.minimum(dr, 2) * 3 + jnp.minimum(dc, 2))
    key_pos = jnp.concatenate([near_pos[slot][:, 0:ATOMS] for slot in slots], axis=1)
    entry = lax.broadcasted_iota(jnp.int32, (1, KEYS), 1) // ATOMS
    own_pos = near_pos[4].T
    square = jnp.zeros((ATOMS, KEYS), F32)
    for c in range(3):
        shift = jnp.zeros((1, KEYS), F32)
        for e in range(8):
            shift = jnp.where(entry == e, offsets[c, 0, e].astype(F32), shift)
        step = (key_pos[c : c + 1, :] + shift - own_pos[0:ATOMS, c : c + 1]) * lengths[c]
        square = square + step * step
    dist[...] = jnp.sqrt(square + 0.25)
    live = jnp.zeros((1, KEYS), jnp.int32)
    for e in range(8):
        live = jnp.where(entry == e, valid[0, e], live)

    first_high, first_low = split(rbf_weight[...])
    shift_high = rbf_offset[...].astype(BF16).astype(F32)
    shift_rest = rbf_offset[...] - shift_high
    shift_mid = shift_rest.astype(BF16).astype(F32)
    which = lax.broadcasted_iota(jnp.int32, (16, 64), 0)
    shift_rows = jnp.where(
        which == 0, shift_high, jnp.where(which == 1, shift_mid, jnp.where(which == 2, shift_rest - shift_mid, 0.0))
    ).astype(BF16)
    first = jnp.concatenate([first_high, first_low, first_high, shift_rows], axis=0)
    second_high, second_low = split(pair_weight[...])
    second = jnp.concatenate([second_high, second_low, second_high], axis=0)
    some = 4

    def pair_step(i, carry):
        reach = jnp.concatenate([dist[pl.ds(i * some + q, 1), :] for q in range(some)], axis=1)
        centres = 2.0 * lax.broadcasted_iota(jnp.int32, (16, some * KEYS), 0).astype(F32)
        away = reach - centres
        high, low = split(jnp.exp(away * away * -0.125))
        ones = jnp.ones((16, some * KEYS), BF16)
        half = 0.5 * tdot(first, jnp.concatenate([high, high, low, ones], axis=0))
        high, low = split(half + half * jnp.tanh(half))
        pair = tdot(second, jnp.concatenate([high, high, low], axis=0))
        for q in range(some):
            bias[pl.ds(pl.multiple_of((i * some + q) * HEADS, HEADS), HEADS), :] = pair[:, q * KEYS : (q + 1) * KEYS]
        return carry

    lax.fori_loop(0, ATOMS // some, pair_step, 0)

    def end_swap(step, carry):
        swap_copy(step).wait_recv()
        return carry

    lax.fori_loop(1, HEADS, end_swap, 0)
    turned = gathered[...].astype(F32).T
    kv[0, 0] = jnp.concatenate([turned[32:64], turned[96:112], turned[64:96]], axis=0).astype(BF16)

    def ring_right(k):
        return remote(kv.at[0, k], kv.at[0, k + 1], ring_send.at[k], ring_recv.at[k + 1], right)

    def ring_left(k):
        source = kv.at[0, RIGHT + k] if not (isinstance(k, int) and k == 0) else kv.at[0, 0]
        return remote(source, kv.at[0, RIGHT + k + 1], ring_send.at[RIGHT + k], ring_recv.at[RIGHT + k + 1], left)

    def across(k):
        return remote(kv.at[0, k], kv.at[1, k], pair_send.at[k], pair_recv.at[k], sibling)

    ring_right(0).start()
    ring_left(0).start()
    across(0).start()

    high, low = split(turned[0:32] * (HEAD**-0.5 * LOG2E))
    wave = turned[96:104] + turned[104:112]
    wave = jnp.where(lax.broadcasted_iota(jnp.int32, (8, GROUP), 0) < 6, wave, 0.0) * (strengths[group] * LOG2E)
    wave_high = wave.astype(BF16).astype(F32)
    zeros = jnp.zeros((8, GROUP), F32)
    queries[...] = jnp.concatenate(
        [
            high,
            jnp.concatenate([wave_high, wave_high], axis=0).astype(BF16),
            low,
            jnp.concatenate([wave - wave_high, zeros], axis=0).astype(BF16),
        ],
        axis=0,
    )
    run_max[...] = jnp.full(run_max.shape, -1e30, F32)
    accum[...] = jnp.zeros(accum.shape, F32)

    def put(slot, side, k):
        part = kv[side, k, 0:48, :]
        scores[slot] = tdot(jnp.concatenate([part, part], axis=0), queries[...])

    def soft(slot, side, k):
        value = scores[slot]
        old = run_max[...]
        new = jnp.maximum(old, jnp.max(value, axis=0, keepdims=True))
        weights = jnp.exp2(value - new).astype(BF16)
        added = jnp.dot(kv[side, k, 32:80, :], weights, preferred_element_type=F32)
        run_max[...] = new
        accum[...] = accum[...] * jnp.exp2(old - new) + added

    put(0, 0, 0)
    halo_copies[0].wait_recv()
    halo_copies[1].wait_recv()
    halo_copies[2].start()
    halo_copies[3].start()
    across(0).wait_recv()
    put(1, 1, 0)
    soft(0, 0, 0)
    ring_right(0).wait_recv()
    ring_right(1).start()
    across(1).start()
    put(0, 0, 1)
    soft(1, 1, 0)

    def ring_step(t, carry):
        ring_left(t - 1).wait_recv()

        @pl.when(t < LEFT)
        def _():
            ring_left(t).start()

        across(RIGHT + t).start()
        put(1, 0, RIGHT + t)
        soft(0, 0, t)
        across(t).wait_recv()
        put(0, 1, t)
        soft(1, 0, RIGHT + t)
        ring_right(t).wait_recv()

        @pl.when(t + 1 < RIGHT)
        def _():
            ring_right(t + 1).start()

        across(t + 1).start()
        across(RIGHT + t).wait_recv()
        put(1, 1, RIGHT + t)
        soft(0, 1, t)
        put(0, 0, t + 1)
        soft(1, 1, RIGHT + t)
        return carry

    lax.fori_loop(1, LEFT + 1, ring_step, 0)
    across(RIGHT).wait_recv()
    put(1, 1, RIGHT)
    soft(0, 0, RIGHT)
    soft(1, 1, RIGHT)

    attended = accum[16:48, :] / accum[6:7, :]
    returning[...] = jnp.concatenate([attended, jnp.zeros((96, GROUP), F32)], axis=0).T.astype(BF16)

    def back_copy(step):
        other, device = plane(step)
        return remote(
            returning.at[pl.ds(pl.multiple_of(other * ATOMS, ATOMS), ATOMS)],
            returned.at[group],
            back_send.at[step],
            back_recv.at[step],
            device,
        )

    def start_back(step, carry):
        back_copy(step).start()
        return carry

    lax.fori_loop(1, HEADS, start_back, 0)
    returned[group] = returning[pl.ds(pl.multiple_of(group * ATOMS, ATOMS), ATOMS), :]

    halo_copies[2].wait_recv()
    halo_copies[3].wait_recv()
    own_head = lax.broadcasted_iota(jnp.int32, (HEADS, WIDTH), 1) // HEAD == lax.broadcasted_iota(
        jnp.int32, (HEADS, WIDTH), 0
    )
    spread_q = jnp.where(own_head[None], own_q[...].astype(F32)[:, None, :], 0.0)
    spread_q = spread_q.reshape(ATOMS * HEADS, WIDTH).astype(BF16)
    near_keys = jnp.concatenate([near_kv[slot][:, :WIDTH] for slot in slots], axis=0)
    near_values = jnp.concatenate([near_kv[slot][:, WIDTH:] for slot in slots], axis=0)
    local = lax.dot_general(spread_q, near_keys, (((1,), (1,)), ((), ())), preferred_element_type=F32)
    local = local * HEAD**-0.5 + bias[...]
    local = jnp.where(live > 0, local, -1e30)
    weights = jnp.exp(local - jnp.max(local, axis=-1, keepdims=True))
    inverse = 1.0 / jnp.sum(weights, axis=-1, keepdims=True)
    mixed = jnp.dot(weights.astype(BF16), near_values, preferred_element_type=F32) * inverse
    mixed = jnp.where(own_head[None], mixed.reshape(ATOMS, HEADS, WIDTH), 0.0)
    local_out = jnp.sum(mixed, axis=1).astype(BF16).astype(F32)

    def end_back(step, carry):
        back_copy(step).wait_recv()
        return carry

    lax.fori_loop(1, HEADS, end_back, 0)
    global_out = jnp.concatenate([returned[head][:, 0:HEAD].astype(F32) for head in range(HEADS)], axis=1)
    combined = (local_out + global_out).astype(BF16)
    updated = floats + jnp.dot(combined, w_out[...], preferred_element_type=F32)
    out[...] = updated.astype(BF16)

    def end_sends(step, carry):
        swap_copy(step).wait_send()
        back_copy(step).wait_send()
        across(step).wait_send()
        return carry

    lax.fori_loop(1, HEADS, end_sends, 0)
    across(0).wait_send()
    for k in range(RIGHT):
        ring_right(k).wait_send()
    for k in range(LEFT):
        ring_left(k).wait_send()
    for k in range(len(moves)):
        pos_copy(k).wait_send()
    for copy in halo_copies:
        copy.wait_send()


def on_device(
    features,
    positions,
    cell_lengths,
    block_lists,
    image_offsets,
    block_valid,
    norm_gain,
    w_qkv,
    w_out,
    rbf_weight,
    rbf_offset,
    pair_weight,
    cosine_scale,
):
    vmem = pl.BlockSpec(memory_space=pltpu.VMEM)
    smem = pl.BlockSpec(memory_space=pltpu.SMEM)
    dma = pltpu.SemaphoreType.DMA
    return pl.pallas_call(
        kernel,
        out_shape=jax.ShapeDtypeStruct((ATOMS, WIDTH), BF16),
        in_specs=[vmem, vmem, smem, smem, smem, smem, vmem, vmem, vmem, vmem, vmem, vmem, smem],
        out_specs=vmem,
        scratch_shapes=[
            pltpu.VMEM((9, ATOMS, 2 * WIDTH), BF16),
            pltpu.VMEM((9, 8, 128), F32),
            pltpu.VMEM((HEADS, ATOMS, 128), BF16),
            pltpu.VMEM((GROUP, 128), BF16),
            pltpu.VMEM((2, 16, 80, GROUP), BF16),
            pltpu.VMEM((96, GROUP), BF16),
            pltpu.VMEM((2, GROUP, GROUP), F32),
            pltpu.VMEM((1, GROUP), F32),
            pltpu.VMEM((48, GROUP), F32),
            pltpu.VMEM((ATOMS, KEYS), F32),
            pltpu.VMEM((ATOMS * HEADS, KEYS), F32),
            pltpu.VMEM((GROUP, 128), BF16),
            pltpu.VMEM((HEADS, ATOMS, 128), BF16),
            pltpu.VMEM((ATOMS, WIDTH), BF16),
            dma((8,)),
            dma((8,)),
            dma((4,)),
            dma((4,)),
            dma((16,)),
            dma((16,)),
            dma((16,)),
            dma((17,)),
            dma((16,)),
            dma((16,)),
            dma((16,)),
            dma((16,)),
        ],
        compiler_params=pltpu.CompilerParams(
            collective_id=0, has_side_effects=True, vmem_limit_bytes=40 * 2**20
        ),
    )(
        features,
        positions,
        cell_lengths,
        block_lists,
        image_offsets,
        block_valid,
        norm_gain.reshape(1, WIDTH),
        w_qkv,
        w_out,
        rbf_weight,
        rbf_offset.reshape(1, 64),
        pair_weight,
        cosine_scale,
    )


def solution(mesh):
    return jax.shard_map(
        on_device,
        mesh=mesh,
        in_specs=(
            P(("rows", "cols"), None),
            P(None, ("rows", "cols")),
            P(),
            P(("rows", "cols"), None),
            P(None, ("rows", "cols"), None),
            P(("rows", "cols"), None),
            P(),
            P(),
            P(),
            P(),
            P(),
            P(),
            P(),
        ),
        out_specs=P(("rows", "cols"), None),
        check_vma=False,
    )
```

```python
import functools
import math

import jax
import jax.numpy as jnp
from jax import lax
from jax.experimental import pallas as pl
from jax.experimental.pallas import tpu as pltpu
from jax.sharding import PartitionSpec as P

MESH = pl.DeviceIdType.MESH
F32 = jnp.float32
BF16 = jnp.bfloat16
LOG2E = math.log2(math.e)

ATOMS = 32
WIDTH = 512
HEADS = 16
HEAD = 32
GROUP = 512
KEYS = 256
ROWS = 16
COLS = 32
DEPTH = 16
SIDE = 4


def tdot(a, b):
    return lax.dot_general(a, b, (((0,), (0,)), ((), ())), preferred_element_type=F32)


def split(value):
    high = value.astype(BF16)
    return high, (value - high.astype(F32)).astype(BF16)


def kernel(
    features_at,
    positions_at,
    lengths_at,
    lists_at,
    offsets_at,
    valid_at,
    gain_at,
    w_qkv_at,
    w_out_at,
    rbf_weight_at,
    rbf_offset_at,
    pair_weight_at,
    strengths_at,
    out,
    features,
    positions,
    lengths,
    lists,
    offsets,
    valid,
    gain,
    w_qkv,
    w_out,
    rbf_weight,
    rbf_offset,
    pair_weight,
    strengths,
    load_sem,
    near_kv,
    near_pos,
    pieces,
    gathered,
    asked,
    kv,
    queries,
    scores,
    run_max,
    accum,
    part_out,
    part_in,
    dist,
    bias,
    returning,
    returned,
    own_q,
    pos_send,
    pos_recv,
    halo_send,
    halo_recv,
    swap_send,
    swap_recv,
    ask_send,
    ask_recv,
    kv_send,
    kv_recv,
    pair_send,
    pair_recv,
    part_send,
    part_recv,
    back_send,
    back_recv,
):
    row, col = lax.axis_index("rows"), lax.axis_index("cols")
    core = lax.rem(row, 2)
    x, y_lo = row // 4, lax.rem(row // 2, 2)
    y_hi, z = col // DEPTH, lax.rem(col, DEPTH)
    y = y_hi * 2 + y_lo

    def line(step):
        other = lax.rem(z + step, HEADS)
        return other, (row, y_hi * DEPTH + other)

    def chip(ox, oy):
        return (ox * 4 + lax.rem(oy, 2) * 2 + core, oy // 2 * DEPTH + z)

    def along_x(step):
        return chip(lax.rem(x + step, SIDE), y)

    def along_y(step):
        return chip(x, lax.rem(y + step, SIDE))

    sibling = (row + 1 - 2 * core, col)

    def beside(dr, dc):
        return (lax.rem(row + dr + ROWS, ROWS), lax.rem(col + dc + COLS, COLS))

    moves = [(dr, dc) for dr in (-1, 0, 1) for dc in (-1, 0, 1) if (dr, dc) != (0, 0)]

    def remote(src, dst, send, recv, device):
        return pltpu.make_async_remote_copy(
            src_ref=src, dst_ref=dst, send_sem=send, recv_sem=recv, device_id=device, device_id_type=MESH
        )

    loads = [
        pltpu.make_async_copy(src, dst, load_sem.at[i])
        for i, (src, dst) in enumerate(
            [
                (w_qkv_at, w_qkv),
                (features_at, features),
                (gain_at, gain),
                (positions_at, positions),
                (strengths_at, strengths),
                (lists_at, lists),
                (offsets_at, offsets),
                (lengths_at, lengths),
                (valid_at, valid),
                (rbf_weight_at, rbf_weight),
                (rbf_offset_at, rbf_offset),
                (pair_weight_at, pair_weight),
                (w_out_at, w_out),
            ]
        )
    ]
    for load in loads:
        load.start()

    barrier = pltpu.get_barrier_semaphore()

    def greet(device):
        pl.semaphore_signal(barrier, inc=1, device_id=device, device_id_type=MESH)

    def greet_line(step, carry):
        greet(line(step)[1])
        return carry

    lax.fori_loop(1, HEADS, greet_line, 0)
    for step in range(1, SIDE):
        greet(along_x(step))
        greet(along_y(step))
    for move in moves:
        greet(beside(*move))
    greet(sibling)

    for load in loads[:4]:
        load.wait()
    pos = positions[...]
    near_pos[4] = jnp.zeros((8, 128), F32)
    near_pos[4, 0:3, 0:ATOMS] = pos
    angles = (2.0 * math.pi) * pos
    waves = jnp.concatenate(
        [jnp.cos(angles), jnp.sin(angles), jnp.ones((1, ATOMS), F32), jnp.zeros((1, ATOMS), F32)], axis=0
    )
    wave_high = waves.astype(BF16).astype(F32)
    waves = jnp.concatenate([wave_high, waves - wave_high], axis=0).astype(BF16)
    place = lax.broadcasted_iota(jnp.int32, (16, 128), 0) + 96 == lax.broadcasted_iota(jnp.int32, (16, 128), 1)
    wave_lanes = tdot(waves, jnp.where(place, 1.0, 0.0).astype(BF16))[:, 96:128]

    floats = features[...].astype(F32)
    spread = jnp.mean(floats * floats, axis=-1, keepdims=True)
    normed = (floats * lax.rsqrt(spread + 1e-06) * gain[...]).astype(BF16)
    packed = jnp.dot(normed, w_qkv[...], preferred_element_type=F32)
    for head in range(HEADS):
        lo = head * HEAD
        pieces[head] = jnp.concatenate(
            [
                packed[:, lo : lo + HEAD],
                packed[:, WIDTH + lo : WIDTH + lo + HEAD],
                packed[:, 2 * WIDTH + lo : 2 * WIDTH + lo + HEAD],
                wave_lanes,
            ],
            axis=1,
        ).astype(BF16)
    own_q[...] = packed[:, :WIDTH].astype(BF16)
    near_kv[4] = packed[:, WIDTH:].astype(BF16)

    pl.semaphore_wait(barrier, HEADS - 1 + 2 * (SIDE - 1) + len(moves) + 1)

    def pos_copy(k):
        dr, dc = moves[k]
        return remote(
            near_pos.at[4],
            near_pos.at[(1 - dr) * 3 + (1 - dc)],
            pos_send.at[k],
            pos_recv.at[k],
            beside(dr, dc),
        )

    def swap_copy(step):
        other, device = line(step)
        return remote(
            pieces.at[other],
            gathered.at[pl.ds(pl.multiple_of(z * ATOMS, ATOMS), ATOMS)],
            swap_send.at[step],
            swap_recv.at[step],
            device,
        )

    def start_swap(step, carry):
        swap_copy(step).start()
        return carry

    lax.fori_loop(1, HEADS, start_swap, 0)
    for k in range(len(moves)):
        pos_copy(k).start()
    gathered[pl.ds(pl.multiple_of(z * ATOMS, ATOMS), ATOMS), :] = pieces[z]

    halo_copies = [
        remote(near_kv.at[4], near_kv.at[3], halo_send.at[0], halo_recv.at[0], beside(0, 1)),
        remote(near_kv.at[4], near_kv.at[5], halo_send.at[1], halo_recv.at[1], beside(0, -1)),
        remote(near_kv.at[pl.ds(3, 3)], near_kv.at[pl.ds(0, 3)], halo_send.at[2], halo_recv.at[2], beside(1, 0)),
        remote(near_kv.at[pl.ds(3, 3)], near_kv.at[pl.ds(6, 3)], halo_send.at[3], halo_recv.at[3], beside(-1, 0)),
    ]
    halo_copies[0].start()
    halo_copies[1].start()

    for load in loads[4:]:
        load.wait()
    for k in range(len(moves)):
        pos_copy(k).wait_recv()
    slots = []
    for e in range(8):
        block = lists[0, e]
        dr = lax.rem(block // COLS - row + 1 + ROWS, ROWS)
        dc = lax.rem(lax.rem(block, COLS) - col + 1 + COLS, COLS)
        slots.append(jnp.minimum(dr, 2) * 3 + jnp.minimum(dc, 2))
    key_pos = jnp.concatenate([near_pos[slot][:, 0:ATOMS] for slot in slots], axis=1)
    entry = lax.broadcasted_iota(jnp.int32, (1, KEYS), 1) // ATOMS
    own_pos = near_pos[4].T
    square = jnp.zeros((ATOMS, KEYS), F32)
    for c in range(3):
        shift = jnp.zeros((1, KEYS), F32)
        for e in range(8):
            shift = jnp.where(entry == e, offsets[c, 0, e].astype(F32), shift)
        step = (key_pos[c : c + 1, :] + shift - own_pos[0:ATOMS, c : c + 1]) * lengths[c]
        square = square + step * step
    dist[...] = jnp.sqrt(square + 0.25)
    live = jnp.zeros((1, KEYS), jnp.int32)
    for e in range(8):
        live = jnp.where(entry == e, valid[0, e], live)

    first_high, first_low = split(rbf_weight[...])
    shift_high = rbf_offset[...].astype(BF16).astype(F32)
    shift_rest = rbf_offset[...] - shift_high
    shift_mid = shift_rest.astype(BF16).astype(F32)
    which = lax.broadcasted_iota(jnp.int32, (16, 64), 0)
    shift_rows = jnp.where(
        which == 0, shift_high, jnp.where(which == 1, shift_mid, jnp.where(which == 2, shift_rest - shift_mid, 0.0))
    ).astype(BF16)
    first = jnp.concatenate([first_high, first_low, first_high, shift_rows], axis=0)
    second = pair_weight[...]
    second_high = second.astype(BF16).astype(F32)
    second = jnp.concatenate([second_high, second - second_high, second_high], axis=1).astype(BF16)
    some = 4

    def pair_step(i, carry):
        reach = jnp.concatenate([dist[pl.ds(i * some + q, 1), :] for q in range(some)], axis=1)
        centres = 2.0 * lax.broadcasted_iota(jnp.int32, (16, some * KEYS), 0).astype(F32)
        away = reach - centres
        high, low = split(jnp.exp(away * away * -0.125))
        ones = jnp.ones((16, some * KEYS), BF16)
        half = 0.5 * tdot(first, jnp.concatenate([high, high, low, ones], axis=0))
        high, low = split(half + half * jnp.tanh(half))
        pair = jnp.dot(second, jnp.concatenate([high, high, low], axis=0), preferred_element_type=F32)
        for q in range(some):
            bias[pl.ds(pl.multiple_of((i * some + q) * HEADS, HEADS), HEADS), :] = pair[:, q * KEYS : (q + 1) * KEYS]
        return carry

    lax.fori_loop(0, ATOMS // some, pair_step, 0)

    halo_copies[0].wait_recv()
    halo_copies[1].wait_recv()
    halo_copies[2].start()
    halo_copies[3].start()

    def end_swap(step, carry):
        swap_copy(step).wait_recv()
        return carry

    lax.fori_loop(1, HEADS, end_swap, 0)
    turned = gathered[...].astype(F32).T
    kv[0, 0] = jnp.concatenate([turned[32:64], turned[96:112], turned[64:96]], axis=0).astype(BF16)
    asked[0] = jnp.concatenate([turned[0:32], turned[96:112]], axis=0).astype(BF16)

    def ask(step, device):
        return remote(asked.at[0], asked.at[step], ask_send.at[step], ask_recv.at[step], device)

    def spread(step, device):
        return remote(kv.at[0, 0], kv.at[0, step], kv_send.at[step], kv_recv.at[step], device)

    def across(step):
        return remote(kv.at[0, step], kv.at[1, step], pair_send.at[step], pair_recv.at[step], sibling)

    across(0).start()
    for step in (1, 3, 2):
        ask(step, along_x(step)).start()
        spread(step, along_y(step)).start()

    def prepare(q):
        rows = asked[q].astype(F32)
        high, low = split(rows[0:32] * (HEAD**-0.5 * LOG2E))
        wave = rows[32:40] + rows[40:48]
        wave = jnp.where(lax.broadcasted_iota(jnp.int32, (8, GROUP), 0) < 6, wave, 0.0) * (strengths[z] * LOG2E)
        wave_high = wave.astype(BF16).astype(F32)
        zeros = jnp.zeros((8, GROUP), F32)
        queries[q] = jnp.concatenate(
            [
                high,
                jnp.concatenate([wave_high, wave_high], axis=0).astype(BF16),
                low,
                jnp.concatenate([wave - wave_high, zeros], axis=0).astype(BF16),
            ],
            axis=0,
        )

    run_max[...] = jnp.full(run_max.shape, -1e30, F32)
    accum[...] = jnp.zeros(accum.shape, F32)

    def put(slot, q, side, k):
        part = kv[side, k, 0:48, :]
        scores[slot] = tdot(jnp.concatenate([part, part], axis=0), queries[q])

    def soft(slot, q, side, k):
        value = scores[slot]
        old = run_max[q]
        new = jnp.maximum(old, jnp.max(value, axis=0, keepdims=True))
        weights = jnp.exp2(value - new).astype(BF16)
        added = jnp.dot(kv[side, k, 32:80, :], weights, preferred_element_type=F32)
        run_max[q] = new
        accum[q] = accum[q] * jnp.exp2(old - new) + added

    def part_copy(q, device):
        return remote(part_out.at[q - 1], part_in.at[q - 1], part_send.at[q - 1], part_recv.at[q - 1], device)

    prepare(0)
    put(0, 0, 0, 0)

    halo_copies[2].wait_recv()
    halo_copies[3].wait_recv()
    own_head = lax.broadcasted_iota(jnp.int32, (HEADS, WIDTH), 1) // HEAD == lax.broadcasted_iota(
        jnp.int32, (HEADS, WIDTH), 0
    )
    spread_q = jnp.where(own_head[None], own_q[...].astype(F32)[:, None, :], 0.0)
    spread_q = spread_q.reshape(ATOMS * HEADS, WIDTH).astype(BF16)
    near_keys = jnp.concatenate([near_kv[slot][:, :WIDTH] for slot in slots], axis=0)
    near_values = jnp.concatenate([near_kv[slot][:, WIDTH:] for slot in slots], axis=0)
    local = lax.dot_general(spread_q, near_keys, (((1,), (1,)), ((), ())), preferred_element_type=F32)
    local = local * HEAD**-0.5 + bias[...]
    local = jnp.where(live > 0, local, -1e30)
    weights = jnp.exp(local - jnp.max(local, axis=-1, keepdims=True))
    inverse = 1.0 / jnp.sum(weights, axis=-1, keepdims=True)
    mixed = jnp.dot(weights.astype(BF16), near_values, preferred_element_type=F32) * inverse
    mixed = jnp.where(own_head[None], mixed.reshape(ATOMS, HEADS, WIDTH), 0.0)
    local_out = jnp.sum(mixed, axis=1).astype(BF16).astype(F32)

    def place_of(p):
        early = p < SIDE
        return (
            jnp.where(early, p, lax.rem((p - SIDE) // 3 + 1 + SIDE, SIDE)),
            jnp.where(early, 0, lax.rem(p - SIDE + SIDE * 3, 3) + 1),
        )

    def unit_step(p, carry):
        q, k = place_of(p)
        next_q, next_k = place_of(lax.rem(p + 1, SIDE * SIDE))

        @pl.when(p == 0)
        def _():
            across(0).wait_recv()

        @pl.when((p >= SIDE) & (p < SIDE + 3))
        def _():
            across(k).wait_recv()

        put(1, q, 1, k)
        soft(0, q, 0, k)

        @pl.when(p < SIDE - 1)
        def _():
            ask(next_q, sibling).wait_recv()
            prepare(next_q)

        @pl.when((p >= 1) & (p < SIDE))
        def _():
            spread(p, sibling).wait_recv()
            across(p).start()

        put(0, next_q, 0, next_k)
        soft(1, q, 1, k)

        @pl.when((p >= SIDE) & (k == 3) & (q > 0))
        def _():
            top = jnp.where(lax.broadcasted_iota(jnp.int32, (8, GROUP), 0) == 0, run_max[q], accum[q, 0:8, :])
            part_out[q - 1] = jnp.concatenate([top, accum[q, 16:48, :]], axis=0)
            part_copy(q, along_x(SIDE - q)).start()

        return carry

    lax.fori_loop(0, SIDE * SIDE, unit_step, 0)

    tops, sums, values = [run_max[0]], [accum[0, 6:7, :]], [accum[0, 16:48, :]]
    for q in range(1, SIDE):
        part_copy(q, sibling).wait_recv()
        part = part_in[q - 1]
        tops.append(part[0:1])
        sums.append(part[6:7])
        values.append(part[8:40])
    top = functools.reduce(jnp.maximum, tops)
    shares = [jnp.exp2(t - top) for t in tops]
    total = sum(share * one for share, one in zip(shares, sums))
    attended = sum(share * one for share, one in zip(shares, values)) / total

    attended = attended.astype(BF16).astype(F32).T.reshape(HEADS, 4, 8, HEAD)
    returning[...] = jnp.concatenate([attended[:, q] for q in range(4)], axis=-1)

    def back_copy(step):
        other, device = line(step)
        return remote(
            returning.at[other],
            returned.at[z],
            back_send.at[step],
            back_recv.at[step],
            device,
        )

    def start_back(step, carry):
        back_copy(step).start()
        return carry

    lax.fori_loop(1, HEADS, start_back, 0)
    returned[z] = returning[z]

    def end_back(step, carry):
        back_copy(step).wait_recv()
        return carry

    lax.fori_loop(1, HEADS, end_back, 0)
    global_out = jnp.concatenate(
        [
            jnp.concatenate([returned[head][:, q * HEAD : (q + 1) * HEAD] for head in range(HEADS)], axis=1)
            for q in range(4)
        ],
        axis=0,
    )
    combined = (local_out + global_out).astype(BF16)
    updated = floats + jnp.dot(combined, w_out[...], preferred_element_type=F32)
    out[...] = updated.astype(BF16)

    def end_sends(step, carry):
        swap_copy(step).wait_send()
        back_copy(step).wait_send()
        return carry

    lax.fori_loop(1, HEADS, end_sends, 0)
    for step in range(SIDE):
        across(step).wait_send()
    for step in range(1, SIDE):
        ask(step, sibling).wait_send()
        spread(step, sibling).wait_send()
        part_copy(step, sibling).wait_send()
    for k in range(len(moves)):
        pos_copy(k).wait_send()
    for copy in halo_copies:
        copy.wait_send()


def on_device(
    features,
    positions,
    cell_lengths,
    block_lists,
    image_offsets,
    block_valid,
    norm_gain,
    w_qkv,
    w_out,
    rbf_weight,
    rbf_offset,
    pair_weight,
    cosine_scale,
):
    hbm = pl.BlockSpec(memory_space=pltpu.HBM)
    dma = pltpu.SemaphoreType.DMA
    return pl.pallas_call(
        kernel,
        out_shape=jax.ShapeDtypeStruct((ATOMS, WIDTH), BF16),
        in_specs=[hbm] * 13,
        out_specs=pl.BlockSpec(memory_space=pltpu.VMEM),
        scratch_shapes=[
            pltpu.VMEM((ATOMS, WIDTH), BF16),
            pltpu.VMEM((3, ATOMS), F32),
            pltpu.SMEM((3,), F32),
            pltpu.SMEM((1, 8), jnp.int32),
            pltpu.SMEM((3, 1, 8), jnp.int32),
            pltpu.SMEM((1, 8), jnp.int32),
            pltpu.VMEM((1, WIDTH), F32),
            pltpu.VMEM((WIDTH, 3 * WIDTH), BF16),
            pltpu.VMEM((WIDTH, WIDTH), BF16),
            pltpu.VMEM((16, 64), F32),
            pltpu.VMEM((1, 64), F32),
            pltpu.VMEM((16, 64), F32),
            pltpu.SMEM((16,), F32),
            dma((13,)),
            pltpu.VMEM((9, ATOMS, 2 * WIDTH), BF16),
            pltpu.VMEM((9, 8, 128), F32),
            pltpu.VMEM((HEADS, ATOMS, 128), BF16),
            pltpu.VMEM((GROUP, 128), BF16),
            pltpu.VMEM((SIDE, 48, GROUP), BF16),
            pltpu.VMEM((2, SIDE, 80, GROUP), BF16),
            pltpu.VMEM((SIDE, 96, GROUP), BF16),
            pltpu.VMEM((2, GROUP, GROUP), F32),
            pltpu.VMEM((SIDE, 1, GROUP), F32),
            pltpu.VMEM((SIDE, 48, GROUP), F32),
            pltpu.VMEM((SIDE - 1, 40, GROUP), F32),
            pltpu.VMEM((SIDE - 1, 40, GROUP), F32),
            pltpu.VMEM((ATOMS, KEYS), F32),
            pltpu.VMEM((ATOMS * HEADS, KEYS), F32),
            pltpu.VMEM((HEADS, 8, 128), F32),
            pltpu.VMEM((HEADS, 8, 128), F32),
            pltpu.VMEM((ATOMS, WIDTH), BF16),
            dma((8,)),
            dma((8,)),
            dma((4,)),
            dma((4,)),
            dma((16,)),
            dma((16,)),
            dma((4,)),
            dma((4,)),
            dma((4,)),
            dma((4,)),
            dma((4,)),
            dma((4,)),
            dma((3,)),
            dma((3,)),
            dma((16,)),
            dma((16,)),
        ],
        compiler_params=pltpu.CompilerParams(
            collective_id=0, has_side_effects=True, vmem_limit_bytes=63 * 2**20
        ),
    )(
        features,
        positions,
        cell_lengths,
        block_lists,
        image_offsets,
        block_valid,
        norm_gain.reshape(1, WIDTH),
        w_qkv,
        w_out,
        rbf_weight,
        rbf_offset.reshape(1, 64),
        pair_weight.T,
        cosine_scale,
    )


def solution(mesh):
    return jax.shard_map(
        on_device,
        mesh=mesh,
        in_specs=(
            P(("rows", "cols"), None),
            P(None, ("rows", "cols")),
            P(),
            P(("rows", "cols"), None),
            P(None, ("rows", "cols"), None),
            P(("rows", "cols"), None),
            P(),
            P(),
            P(),
            P(),
            P(),
            P(),
            P(),
        ),
        out_specs=P(("rows", "cols"), None),
        check_vma=False,
    )
```

```python
import functools
import math

import jax
import jax.numpy as jnp
from jax import lax
from jax.experimental import pallas as pl
from jax.experimental.pallas import tpu as pltpu
from jax.sharding import PartitionSpec as P

MESH = pl.DeviceIdType.MESH
F32 = jnp.float32
BF16 = jnp.bfloat16
LOG2E = math.log2(math.e)

ATOMS = 32
WIDTH = 512
HEADS = 16
HEAD = 32
GROUP = 512
KEYS = 256
ROWS = 16
COLS = 32
DEPTH = 16
RIGHT = 8


def tdot(a, b):
    return lax.dot_general(a, b, (((0,), (0,)), ((), ())), preferred_element_type=F32)


def split(value):
    high = value.astype(BF16)
    return high, (value - high.astype(F32)).astype(BF16)


def kernel(
    features_at,
    positions_at,
    lengths_at,
    lists_at,
    offsets_at,
    valid_at,
    gain_at,
    w_qkv_at,
    w_out_at,
    rbf_weight_at,
    rbf_offset_at,
    pair_weight_at,
    strengths_at,
    out,
    features,
    positions,
    lengths,
    lists,
    offsets,
    valid,
    gain,
    w_qkv,
    w_out,
    rbf_weight,
    rbf_offset,
    pair_weight,
    strengths,
    load_sem,
    near_kv,
    near_pos,
    pieces,
    gathered,
    asked,
    kv,
    queries,
    scores,
    run_max,
    accum,
    part_out,
    part_in,
    dist,
    bias,
    returning,
    returned,
    own_q,
    pos_send,
    pos_recv,
    halo_send,
    halo_recv,
    swap_send,
    swap_recv,
    ask_send,
    ask_recv,
    kv_send,
    kv_recv,
    part_send,
    part_recv,
    back_send,
    back_recv,
):
    row, col = lax.axis_index("rows"), lax.axis_index("cols")
    core = lax.rem(row, 2)
    x, y_lo = row // 4, lax.rem(row // 2, 2)
    y_hi, z = col // DEPTH, lax.rem(col, DEPTH)
    y = y_hi * 2 + y_lo

    head_here = x * 4 + y

    def plane(step):
        other = lax.rem(head_here + step, HEADS)
        oy = lax.rem(other, 4)
        return other, (other // 4 * 4 + lax.rem(oy, 2) * 2 + core, oy // 2 * DEPTH + z)

    def along_z(step):
        return (row, y_hi * DEPTH + lax.rem(z + step + DEPTH, DEPTH))

    sibling = (row + 1 - 2 * core, col)

    def beside(dr, dc):
        return (lax.rem(row + dr + ROWS, ROWS), lax.rem(col + dc + COLS, COLS))

    moves = [(dr, dc) for dr in (-1, 0, 1) for dc in (-1, 0, 1) if (dr, dc) != (0, 0)]

    def remote(src, dst, send, recv, device):
        return pltpu.make_async_remote_copy(
            src_ref=src, dst_ref=dst, send_sem=send, recv_sem=recv, device_id=device, device_id_type=MESH
        )

    loads = [
        pltpu.make_async_copy(src, dst, load_sem.at[i])
        for i, (src, dst) in enumerate(
            [
                (w_qkv_at, w_qkv),
                (features_at, features),
                (gain_at, gain),
                (positions_at, positions),
                (strengths_at, strengths),
                (lists_at, lists),
                (offsets_at, offsets),
                (lengths_at, lengths),
                (valid_at, valid),
                (rbf_weight_at, rbf_weight),
                (rbf_offset_at, rbf_offset),
                (pair_weight_at, pair_weight),
                (w_out_at, w_out),
            ]
        )
    ]
    for load in loads:
        load.start()

    barrier = pltpu.get_barrier_semaphore()

    def greet(device):
        pl.semaphore_signal(barrier, inc=1, device_id=device, device_id_type=MESH)

    def greet_plane(step, carry):
        greet(plane(step)[1])
        return carry

    lax.fori_loop(1, HEADS, greet_plane, 0)
    for step in (-2, -1, 1, 2):
        greet(along_z(step))
    for move in moves:
        greet(beside(*move))
    greet(sibling)

    for load in loads[:4]:
        load.wait()
    pos = positions[...]
    near_pos[4] = jnp.zeros((8, 128), F32)
    near_pos[4, 0:3, 0:ATOMS] = pos
    angles = (2.0 * math.pi) * pos
    waves = jnp.concatenate(
        [jnp.cos(angles), jnp.sin(angles), jnp.ones((1, ATOMS), F32), jnp.zeros((1, ATOMS), F32)], axis=0
    )
    wave_high = waves.astype(BF16).astype(F32)
    waves = jnp.concatenate([wave_high, waves - wave_high], axis=0).astype(BF16)
    place = lax.broadcasted_iota(jnp.int32, (16, 128), 0) + 96 == lax.broadcasted_iota(jnp.int32, (16, 128), 1)
    wave_lanes = tdot(waves, jnp.where(place, 1.0, 0.0).astype(BF16))[:, 96:128]

    floats = features[...].astype(F32)
    spread = jnp.mean(floats * floats, axis=-1, keepdims=True)
    normed = (floats * lax.rsqrt(spread + 1e-06) * gain[...]).astype(BF16)
    packed = jnp.dot(normed, w_qkv[...], preferred_element_type=F32)
    for head in range(HEADS):
        lo = head * HEAD
        pieces[head] = jnp.concatenate(
            [
                packed[:, lo : lo + HEAD],
                packed[:, WIDTH + lo : WIDTH + lo + HEAD],
                packed[:, 2 * WIDTH + lo : 2 * WIDTH + lo + HEAD],
                wave_lanes,
            ],
            axis=1,
        ).astype(BF16)
    own_q[...] = packed[:, :WIDTH].astype(BF16)
    near_kv[4] = packed[:, WIDTH:].astype(BF16)

    pl.semaphore_wait(barrier, HEADS - 1 + 4 + len(moves) + 1)

    def pos_copy(k):
        dr, dc = moves[k]
        return remote(
            near_pos.at[4],
            near_pos.at[(1 - dr) * 3 + (1 - dc)],
            pos_send.at[k],
            pos_recv.at[k],
            beside(dr, dc),
        )

    def swap_copy(step):
        other, device = plane(step)
        return remote(
            pieces.at[other],
            gathered.at[pl.ds(pl.multiple_of(head_here * ATOMS, ATOMS), ATOMS)],
            swap_send.at[step],
            swap_recv.at[step],
            device,
        )

    def start_swap(step, carry):
        swap_copy(step).start()
        return carry

    lax.fori_loop(1, HEADS, start_swap, 0)
    for k in range(len(moves)):
        pos_copy(k).start()
    gathered[pl.ds(pl.multiple_of(head_here * ATOMS, ATOMS), ATOMS), :] = pieces[head_here]

    halo_copies = [
        remote(near_kv.at[4], near_kv.at[3], halo_send.at[0], halo_recv.at[0], beside(0, 1)),
        remote(near_kv.at[4], near_kv.at[5], halo_send.at[1], halo_recv.at[1], beside(0, -1)),
        remote(near_kv.at[pl.ds(3, 3)], near_kv.at[pl.ds(0, 3)], halo_send.at[2], halo_recv.at[2], beside(1, 0)),
        remote(near_kv.at[pl.ds(3, 3)], near_kv.at[pl.ds(6, 3)], halo_send.at[3], halo_recv.at[3], beside(-1, 0)),
    ]
    halo_copies[0].start()
    halo_copies[1].start()

    for load in loads[4:]:
        load.wait()

    def end_swap(step, carry):
        swap_copy(step).wait_recv()
        return carry

    lax.fori_loop(1, HEADS, end_swap, 0)
    turned = gathered[...].astype(F32).T
    kv[0] = jnp.concatenate([turned[32:64], turned[96:112], turned[64:96]], axis=0).astype(BF16)
    asked[0] = jnp.concatenate([turned[0:32], turned[96:112]], axis=0).astype(BF16)

    def hand(source, target, device):
        return remote(kv.at[source], kv.at[target], kv_send.at[target], kv_recv.at[target], device)

    hand(0, 2, along_z(2)).start()
    hand(0, RIGHT + 2, along_z(-2)).start()
    ask = remote(asked.at[0], asked.at[1], ask_send, ask_recv, sibling)
    ask.start()
    hand(0, 1, along_z(1)).start()
    hand(0, RIGHT + 1, along_z(-1)).start()

    def prepare(q):
        rows = asked[q].astype(F32)
        high, low = split(rows[0:32] * (HEAD**-0.5 * LOG2E))
        wave = rows[32:40] + rows[40:48]
        wave = jnp.where(lax.broadcasted_iota(jnp.int32, (8, GROUP), 0) < 6, wave, 0.0) * (strengths[head_here] * LOG2E)
        wave_high = wave.astype(BF16).astype(F32)
        zeros = jnp.zeros((8, GROUP), F32)
        queries[q] = jnp.concatenate(
            [
                high,
                jnp.concatenate([wave_high, wave_high], axis=0).astype(BF16),
                low,
                jnp.concatenate([wave - wave_high, zeros], axis=0).astype(BF16),
            ],
            axis=0,
        )

    run_max[...] = jnp.full(run_max.shape, -1e30, F32)
    accum[...] = jnp.zeros(accum.shape, F32)

    def put(slot, q, k):
        part = kv[k, 0:48, :]
        scores[slot] = tdot(jnp.concatenate([part, part], axis=0), queries[q])

    def soft(slot, q, k):
        value = scores[slot]
        old = run_max[q]
        new = jnp.maximum(old, jnp.max(value, axis=0, keepdims=True))
        weights = jnp.exp2(value - new).astype(BF16)
        added = jnp.dot(kv[k, 32:80, :], weights, preferred_element_type=F32)
        run_max[q] = new
        accum[q] = accum[q] * jnp.exp2(old - new) + added

    def attend(units):
        put(0, *units[0])
        for i, unit in enumerate(units):
            if i + 1 < len(units):
                put((i + 1) % 2, *units[i + 1])
            soft(i % 2, *unit)

    prepare(0)
    attend([(0, 0)])
    halo_copies[0].wait_recv()
    halo_copies[1].wait_recv()
    halo_copies[2].start()
    halo_copies[3].start()

    for k in range(len(moves)):
        pos_copy(k).wait_recv()
    slots = []
    for e in range(8):
        block = lists[0, e]
        dr = lax.rem(block // COLS - row + 1 + ROWS, ROWS)
        dc = lax.rem(lax.rem(block, COLS) - col + 1 + COLS, COLS)
        slots.append(jnp.minimum(dr, 2) * 3 + jnp.minimum(dc, 2))
    key_pos = jnp.concatenate([near_pos[slot][:, 0:ATOMS] for slot in slots], axis=1)
    entry = lax.broadcasted_iota(jnp.int32, (1, KEYS), 1) // ATOMS
    own_pos = near_pos[4].T
    square = jnp.zeros((ATOMS, KEYS), F32)
    for c in range(3):
        shift = jnp.zeros((1, KEYS), F32)
        for e in range(8):
            shift = jnp.where(entry == e, offsets[c, 0, e].astype(F32), shift)
        step = (key_pos[c : c + 1, :] + shift - own_pos[0:ATOMS, c : c + 1]) * lengths[c]
        square = square + step * step
    dist[...] = jnp.sqrt(square + 0.25)
    live = jnp.zeros((1, KEYS), jnp.int32)
    for e in range(8):
        live = jnp.where(entry == e, valid[0, e], live)

    first_high, first_low = split(rbf_weight[...])
    shift_high = rbf_offset[...].astype(BF16).astype(F32)
    shift_rest = rbf_offset[...] - shift_high
    shift_mid = shift_rest.astype(BF16).astype(F32)
    which = lax.broadcasted_iota(jnp.int32, (16, 64), 0)
    shift_rows = jnp.where(
        which == 0, shift_high, jnp.where(which == 1, shift_mid, jnp.where(which == 2, shift_rest - shift_mid, 0.0))
    ).astype(BF16)
    first = jnp.concatenate([first_high, first_low, first_high, shift_rows], axis=0)
    second = pair_weight[...]
    second_high = second.astype(BF16).astype(F32)
    second = jnp.concatenate([second_high, second - second_high, second_high], axis=1).astype(BF16)
    some = 4

    def pair_step(i, carry):
        reach = jnp.concatenate([dist[pl.ds(i * some + q, 1), :] for q in range(some)], axis=1)
        centres = 2.0 * lax.broadcasted_iota(jnp.int32, (16, some * KEYS), 0).astype(F32)
        away = reach - centres
        high, low = split(jnp.exp(away * away * -0.125))
        ones = jnp.ones((16, some * KEYS), BF16)
        half = 0.5 * tdot(first, jnp.concatenate([high, high, low, ones], axis=0))
        high, low = split(half + half * jnp.tanh(half))
        pair = jnp.dot(second, jnp.concatenate([high, high, low], axis=0), preferred_element_type=F32)
        for q in range(some):
            bias[pl.ds(pl.multiple_of((i * some + q) * HEADS, HEADS), HEADS), :] = pair[:, q * KEYS : (q + 1) * KEYS]
        return carry

    lax.fori_loop(0, ATOMS // some, pair_step, 0)

    ask.wait_recv()
    prepare(1)
    attend([(1, 0)])

    def relay_step(t, carry):
        near, far = 2 * t + 1, 2 * t + 2
        hand(0, far, sibling).wait_recv()
        hand(far, far + 2, along_z(2)).start()
        hand(far, far + 1, along_z(1)).start()
        hand(0, RIGHT + far, sibling).wait_recv()

        @pl.when(t < 2)
        def _():
            hand(RIGHT + far, RIGHT + far + 2, along_z(-2)).start()

        hand(RIGHT + far, RIGHT + far + 1, along_z(-1)).start()
        hand(0, near, sibling).wait_recv()
        hand(0, RIGHT + near, sibling).wait_recv()
        attend([(q, k) for k in (far, RIGHT + far, near, RIGHT + near) for q in (0, 1)])
        return carry

    lax.fori_loop(0, 3, relay_step, 0)

    halo_copies[2].wait_recv()
    halo_copies[3].wait_recv()
    own_head = lax.broadcasted_iota(jnp.int32, (HEADS, WIDTH), 1) // HEAD == lax.broadcasted_iota(
        jnp.int32, (HEADS, WIDTH), 0
    )
    spread_q = jnp.where(own_head[None], own_q[...].astype(F32)[:, None, :], 0.0)
    spread_q = spread_q.reshape(ATOMS * HEADS, WIDTH).astype(BF16)
    near_keys = jnp.concatenate([near_kv[slot][:, :WIDTH] for slot in slots], axis=0)
    near_values = jnp.concatenate([near_kv[slot][:, WIDTH:] for slot in slots], axis=0)
    local = lax.dot_general(spread_q, near_keys, (((1,), (1,)), ((), ())), preferred_element_type=F32)
    local = local * HEAD**-0.5 + bias[...]
    local = jnp.where(live > 0, local, -1e30)
    weights = jnp.exp(local - jnp.max(local, axis=-1, keepdims=True))
    inverse = 1.0 / jnp.sum(weights, axis=-1, keepdims=True)
    mixed = jnp.dot(weights.astype(BF16), near_values, preferred_element_type=F32) * inverse
    mixed = jnp.where(own_head[None], mixed.reshape(ATOMS, HEADS, WIDTH), 0.0)
    local_out = jnp.sum(mixed, axis=1).astype(BF16).astype(F32)

    last = (RIGHT - 1, DEPTH - 1, RIGHT)
    for k in last:
        hand(0, k, sibling).wait_recv()
    attend([(1, k) for k in last])
    head_rows = jnp.where(lax.broadcasted_iota(jnp.int32, (8, GROUP), 0) == 0, run_max[1], accum[1, 0:8, :])
    part_out[...] = jnp.concatenate([head_rows, accum[1, 16:48, :]], axis=0)
    give = remote(part_out, part_in, part_send, part_recv, sibling)
    give.start()
    attend([(0, k) for k in last])

    give.wait_recv()
    part = part_in[...]
    tops = [run_max[0], part[0:1]]
    sums = [accum[0, 6:7, :], part[6:7]]
    values = [accum[0, 16:48, :], part[8:40]]
    top = functools.reduce(jnp.maximum, tops)
    shares = [jnp.exp2(t - top) for t in tops]
    total = sum(share * one for share, one in zip(shares, sums))
    attended = sum(share * one for share, one in zip(shares, values)) / total

    attended = attended.astype(BF16).astype(F32).T.reshape(HEADS, 4, 8, HEAD)
    returning[...] = jnp.concatenate([attended[:, q] for q in range(4)], axis=-1)

    def back_copy(step):
        other, device = plane(step)
        return remote(
            returning.at[other],
            returned.at[head_here],
            back_send.at[step],
            back_recv.at[step],
            device,
        )

    def start_back(step, carry):
        back_copy(step).start()
        return carry

    lax.fori_loop(1, HEADS, start_back, 0)
    returned[head_here] = returning[head_here]

    def end_back(step, carry):
        back_copy(step).wait_recv()
        return carry

    lax.fori_loop(1, HEADS, end_back, 0)
    global_out = jnp.concatenate(
        [
            jnp.concatenate([returned[head][:, q * HEAD : (q + 1) * HEAD] for head in range(HEADS)], axis=1)
            for q in range(4)
        ],
        axis=0,
    )
    combined = (local_out + global_out).astype(BF16)
    updated = floats + jnp.dot(combined, w_out[...], preferred_element_type=F32)
    out[...] = updated.astype(BF16)

    def end_sends(step, carry):
        swap_copy(step).wait_send()
        back_copy(step).wait_send()
        hand(0, step, sibling).wait_send()
        return carry

    lax.fori_loop(1, HEADS, end_sends, 0)
    ask.wait_send()
    give.wait_send()
    for k in range(len(moves)):
        pos_copy(k).wait_send()
    for copy in halo_copies:
        copy.wait_send()


def on_device(
    features,
    positions,
    cell_lengths,
    block_lists,
    image_offsets,
    block_valid,
    norm_gain,
    w_qkv,
    w_out,
    rbf_weight,
    rbf_offset,
    pair_weight,
    cosine_scale,
):
    hbm = pl.BlockSpec(memory_space=pltpu.HBM)
    dma = pltpu.SemaphoreType.DMA
    return pl.pallas_call(
        kernel,
        out_shape=jax.ShapeDtypeStruct((ATOMS, WIDTH), BF16),
        in_specs=[hbm] * 13,
        out_specs=pl.BlockSpec(memory_space=pltpu.VMEM),
        scratch_shapes=[
            pltpu.VMEM((ATOMS, WIDTH), BF16),
            pltpu.VMEM((3, ATOMS), F32),
            pltpu.SMEM((3,), F32),
            pltpu.SMEM((1, 8), jnp.int32),
            pltpu.SMEM((3, 1, 8), jnp.int32),
            pltpu.SMEM((1, 8), jnp.int32),
            pltpu.VMEM((1, WIDTH), F32),
            pltpu.VMEM((WIDTH, 3 * WIDTH), BF16),
            pltpu.VMEM((WIDTH, WIDTH), BF16),
            pltpu.VMEM((16, 64), F32),
            pltpu.VMEM((1, 64), F32),
            pltpu.VMEM((16, 64), F32),
            pltpu.SMEM((16,), F32),
            dma((13,)),
            pltpu.VMEM((9, ATOMS, 2 * WIDTH), BF16),
            pltpu.VMEM((9, 8, 128), F32),
            pltpu.VMEM((HEADS, ATOMS, 128), BF16),
            pltpu.VMEM((GROUP, 128), BF16),
            pltpu.VMEM((2, 48, GROUP), BF16),
            pltpu.VMEM((DEPTH, 80, GROUP), BF16),
            pltpu.VMEM((2, 96, GROUP), BF16),
            pltpu.VMEM((2, GROUP, GROUP), F32),
            pltpu.VMEM((2, 1, GROUP), F32),
            pltpu.VMEM((2, 48, GROUP), F32),
            pltpu.VMEM((40, GROUP), F32),
            pltpu.VMEM((40, GROUP), F32),
            pltpu.VMEM((ATOMS, KEYS), F32),
            pltpu.VMEM((ATOMS * HEADS, KEYS), F32),
            pltpu.VMEM((HEADS, 8, 128), F32),
            pltpu.VMEM((HEADS, 8, 128), F32),
            pltpu.VMEM((ATOMS, WIDTH), BF16),
            dma((8,)),
            dma((8,)),
            dma((4,)),
            dma((4,)),
            dma((16,)),
            dma((16,)),
            dma(()),
            dma(()),
            dma((16,)),
            dma((16,)),
            dma(()),
            dma(()),
            dma((16,)),
            dma((16,)),
        ],
        compiler_params=pltpu.CompilerParams(
            collective_id=0, has_side_effects=True, vmem_limit_bytes=63 * 2**20
        ),
    )(
        features,
        positions,
        cell_lengths,
        block_lists,
        image_offsets,
        block_valid,
        norm_gain.reshape(1, WIDTH),
        w_qkv,
        w_out,
        rbf_weight,
        rbf_offset.reshape(1, 64),
        pair_weight.T,
        cosine_scale,
    )


def solution(mesh):
    return jax.shard_map(
        on_device,
        mesh=mesh,
        in_specs=(
            P(("rows", "cols"), None),
            P(None, ("rows", "cols")),
            P(),
            P(("rows", "cols"), None),
            P(None, ("rows", "cols"), None),
            P(("rows", "cols"), None),
            P(),
            P(),
            P(),
            P(),
            P(),
            P(),
            P(),
        ),
        out_specs=P(("rows", "cols"), None),
        check_vma=False,
    )
```

```python
import functools
import math

import jax
import jax.numpy as jnp
from jax import lax
from jax.experimental import pallas as pl
from jax.experimental.pallas import tpu as pltpu
from jax.sharding import PartitionSpec as P

MESH = pl.DeviceIdType.MESH
F32 = jnp.float32
BF16 = jnp.bfloat16
LOG2E = math.log2(math.e)

ATOMS = 32
WIDTH = 512
HEADS = 16
HEAD = 32
GROUP = 512
KEYS = 256
ROWS = 16
COLS = 32
DEPTH = 16
RIGHT = 8


def tdot(a, b):
    return lax.dot_general(a, b, (((0,), (0,)), ((), ())), preferred_element_type=F32)


def split(value):
    high = value.astype(BF16)
    return high, (value - high.astype(F32)).astype(BF16)


def kernel(
    features_at,
    positions_at,
    lengths_at,
    lists_at,
    offsets_at,
    valid_at,
    gain_at,
    w_qkv_at,
    w_out_at,
    rbf_weight_at,
    rbf_offset_at,
    pair_weight_at,
    strengths_at,
    out,
    features,
    positions,
    lengths,
    lists,
    offsets,
    valid,
    gain,
    w_qkv,
    w_out,
    rbf_weight,
    rbf_offset,
    pair_weight,
    strengths,
    load_sem,
    near_kv,
    near_pos,
    pieces,
    gathered,
    asked,
    kv,
    queries,
    scores,
    run_max,
    accum,
    part_out,
    part_in,
    dist,
    bias,
    returning,
    returned,
    own_q,
    pos_send,
    pos_recv,
    halo_send,
    halo_recv,
    swap_send,
    swap_recv,
    ask_send,
    ask_recv,
    kv_send,
    kv_recv,
    part_send,
    part_recv,
    back_send,
    back_recv,
):
    row, col = lax.axis_index("rows"), lax.axis_index("cols")
    core = lax.rem(row, 2)
    x, y_lo = row // 4, lax.rem(row // 2, 2)
    y_hi, z = col // DEPTH, lax.rem(col, DEPTH)
    y = y_hi * 2 + y_lo

    head_here = x * 4 + y

    def plane(step):
        other = lax.rem(head_here + step, HEADS)
        oy = lax.rem(other, 4)
        return other, (other // 4 * 4 + lax.rem(oy, 2) * 2 + core, oy // 2 * DEPTH + z)

    def along_z(step):
        return (row, y_hi * DEPTH + lax.rem(z + step + DEPTH, DEPTH))

    sibling = (row + 1 - 2 * core, col)

    def beside(dr, dc):
        return (lax.rem(row + dr + ROWS, ROWS), lax.rem(col + dc + COLS, COLS))

    moves = [(dr, dc) for dr in (-1, 0, 1) for dc in (-1, 0, 1) if (dr, dc) != (0, 0)]

    def remote(src, dst, send, recv, device):
        return pltpu.make_async_remote_copy(
            src_ref=src, dst_ref=dst, send_sem=send, recv_sem=recv, device_id=device, device_id_type=MESH
        )

    loads = [
        pltpu.make_async_copy(src, dst, load_sem.at[i])
        for i, (src, dst) in enumerate(
            [
                (w_qkv_at, w_qkv),
                (features_at, features),
                (gain_at, gain),
                (positions_at, positions),
                (strengths_at, strengths),
                (lists_at, lists),
                (offsets_at, offsets),
                (lengths_at, lengths),
                (valid_at, valid),
                (rbf_weight_at, rbf_weight),
                (rbf_offset_at, rbf_offset),
                (pair_weight_at, pair_weight),
                (w_out_at, w_out),
            ]
        )
    ]
    for load in loads[:4]:
        load.start()

    barrier = pltpu.get_barrier_semaphore()

    def greet(device):
        pl.semaphore_signal(barrier, inc=1, device_id=device, device_id_type=MESH)

    def greet_plane(step, carry):
        greet(plane(step)[1])
        return carry

    lax.fori_loop(1, HEADS, greet_plane, 0)
    for step in (-2, -1, 1, 2):
        greet(along_z(step))
    for move in moves:
        greet(beside(*move))
    greet(sibling)
    for load in loads[4:]:
        load.start()

    for load in loads[:4]:
        load.wait()
    pos = positions[...]
    near_pos[4] = jnp.zeros((8, 128), F32)
    near_pos[4, 0:3, 0:ATOMS] = pos
    angles = (2.0 * math.pi) * pos
    waves = jnp.concatenate(
        [jnp.cos(angles), jnp.sin(angles), jnp.ones((1, ATOMS), F32), jnp.zeros((1, ATOMS), F32)], axis=0
    )
    wave_high = waves.astype(BF16).astype(F32)
    waves = jnp.concatenate([wave_high, waves - wave_high], axis=0).astype(BF16)
    place = lax.broadcasted_iota(jnp.int32, (16, 128), 0) + 96 == lax.broadcasted_iota(jnp.int32, (16, 128), 1)
    wave_lanes = tdot(waves, jnp.where(place, 1.0, 0.0).astype(BF16))[:, 96:128]

    floats = features[...].astype(F32)
    spread = jnp.mean(floats * floats, axis=-1, keepdims=True)
    normed = (floats * lax.rsqrt(spread + 1e-06) * gain[...]).astype(BF16)
    packed = jnp.dot(normed, w_qkv[...], preferred_element_type=F32)
    for head in range(HEADS):
        lo = head * HEAD
        pieces[head] = jnp.concatenate(
            [
                packed[:, lo : lo + HEAD],
                packed[:, WIDTH + lo : WIDTH + lo + HEAD],
                packed[:, 2 * WIDTH + lo : 2 * WIDTH + lo + HEAD],
                wave_lanes,
            ],
            axis=1,
        ).astype(BF16)
    own_q[...] = packed[:, :WIDTH].astype(BF16)
    near_kv[4] = packed[:, WIDTH:].astype(BF16)

    pl.semaphore_wait(barrier, HEADS - 1 + 4 + len(moves) + 1)

    def pos_copy(k):
        dr, dc = moves[k]
        return remote(
            near_pos.at[4],
            near_pos.at[(1 - dr) * 3 + (1 - dc)],
            pos_send.at[k],
            pos_recv.at[k],
            beside(dr, dc),
        )

    def swap_copy(step):
        other, device = plane(step)
        return remote(
            pieces.at[other],
            gathered.at[pl.ds(pl.multiple_of(head_here * ATOMS, ATOMS), ATOMS)],
            swap_send.at[step],
            swap_recv.at[step],
            device,
        )

    def start_swap(step, carry):
        swap_copy(step).start()
        return carry

    lax.fori_loop(1, HEADS, start_swap, 0)
    for k in range(len(moves)):
        pos_copy(k).start()
    gathered[pl.ds(pl.multiple_of(head_here * ATOMS, ATOMS), ATOMS), :] = pieces[head_here]

    halo_copies = [
        remote(near_kv.at[4], near_kv.at[3], halo_send.at[0], halo_recv.at[0], beside(0, 1)),
        remote(near_kv.at[4], near_kv.at[5], halo_send.at[1], halo_recv.at[1], beside(0, -1)),
        remote(near_kv.at[pl.ds(3, 3)], near_kv.at[pl.ds(0, 3)], halo_send.at[2], halo_recv.at[2], beside(1, 0)),
        remote(near_kv.at[pl.ds(3, 3)], near_kv.at[pl.ds(6, 3)], halo_send.at[3], halo_recv.at[3], beside(-1, 0)),
    ]
    halo_copies[0].start()
    halo_copies[1].start()

    for load in loads[4:]:
        load.wait()

    def end_swap(step, carry):
        swap_copy(step).wait_recv()
        return carry

    lax.fori_loop(1, HEADS, end_swap, 0)
    turned = gathered[...].astype(F32).T
    kv[0] = jnp.concatenate([turned[32:64], turned[96:112], turned[64:96]], axis=0).astype(BF16)
    asked[0] = jnp.concatenate([turned[0:32], turned[96:112]], axis=0).astype(BF16)

    def hand(source, target, part, device):
        rows = pl.ds(0, 48) if part == 0 else pl.ds(48, 32)
        return remote(
            kv.at[source, rows], kv.at[target, rows], kv_send.at[part, target], kv_recv.at[part, target], device
        )

    def have(target):
        for part in range(2):
            hand(0, target, part, sibling).wait_recv()

    for part in range(2):
        hand(0, 2, part, along_z(2)).start()
        hand(0, RIGHT + 2, part, along_z(-2)).start()
    ask = remote(asked.at[0], asked.at[1], ask_send, ask_recv, sibling)
    ask.start()
    for part in range(2):
        hand(0, 1, part, along_z(1)).start()
        hand(0, RIGHT + 1, part, along_z(-1)).start()

    def prepare(q):
        rows = asked[q].astype(F32)
        high, low = split(rows[0:32] * (HEAD**-0.5 * LOG2E))
        wave = rows[32:40] + rows[40:48]
        wave = jnp.where(lax.broadcasted_iota(jnp.int32, (8, GROUP), 0) < 6, wave, 0.0) * (strengths[head_here] * LOG2E)
        wave_high = wave.astype(BF16).astype(F32)
        zeros = jnp.zeros((8, GROUP), F32)
        queries[q] = jnp.concatenate(
            [
                high,
                jnp.concatenate([wave_high, wave_high], axis=0).astype(BF16),
                low,
                jnp.concatenate([wave - wave_high, zeros], axis=0).astype(BF16),
            ],
            axis=0,
        )

    run_max[...] = jnp.full(run_max.shape, -1e30, F32)
    accum[...] = jnp.zeros(accum.shape, F32)

    def put(slot, q, k):
        part = kv[k, 0:48, :]
        scores[slot] = tdot(jnp.concatenate([part, part], axis=0), queries[q])

    def soft(slot, q, k):
        value = scores[slot]
        old = run_max[q]
        new = jnp.maximum(old, jnp.max(value, axis=0, keepdims=True))
        weights = jnp.exp2(value - new).astype(BF16)
        added = jnp.dot(kv[k, 32:80, :], weights, preferred_element_type=F32)
        run_max[q] = new
        accum[q] = accum[q] * jnp.exp2(old - new) + added

    def attend(units):
        put(0, *units[0])
        for i, unit in enumerate(units):
            if i + 1 < len(units):
                put((i + 1) % 2, *units[i + 1])
            soft(i % 2, *unit)

    prepare(0)
    attend([(0, 0)])
    halo_copies[0].wait_recv()
    halo_copies[1].wait_recv()
    halo_copies[2].start()
    halo_copies[3].start()

    for k in range(len(moves)):
        pos_copy(k).wait_recv()
    slots = []
    for e in range(8):
        block = lists[0, e]
        dr = lax.rem(block // COLS - row + 1 + ROWS, ROWS)
        dc = lax.rem(lax.rem(block, COLS) - col + 1 + COLS, COLS)
        slots.append(jnp.minimum(dr, 2) * 3 + jnp.minimum(dc, 2))
    key_pos = jnp.concatenate([near_pos[slot][:, 0:ATOMS] for slot in slots], axis=1)
    entry = lax.broadcasted_iota(jnp.int32, (1, KEYS), 1) // ATOMS
    own_pos = near_pos[4].T
    square = jnp.zeros((ATOMS, KEYS), F32)
    for c in range(3):
        shift = jnp.zeros((1, KEYS), F32)
        for e in range(8):
            shift = jnp.where(entry == e, offsets[c, 0, e].astype(F32), shift)
        step = (key_pos[c : c + 1, :] + shift - own_pos[0:ATOMS, c : c + 1]) * lengths[c]
        square = square + step * step
    dist[...] = jnp.sqrt(square + 0.25)
    live = jnp.zeros((1, KEYS), jnp.int32)
    for e in range(8):
        live = jnp.where(entry == e, valid[0, e], live)

    first_high, first_low = split(rbf_weight[...])
    shift_high = rbf_offset[...].astype(BF16).astype(F32)
    shift_rest = rbf_offset[...] - shift_high
    shift_mid = shift_rest.astype(BF16).astype(F32)
    which = lax.broadcasted_iota(jnp.int32, (16, 64), 0)
    shift_rows = jnp.where(
        which == 0, shift_high, jnp.where(which == 1, shift_mid, jnp.where(which == 2, shift_rest - shift_mid, 0.0))
    ).astype(BF16)
    first = jnp.concatenate([first_high, first_low, first_high, shift_rows], axis=0)
    second = pair_weight[...]
    second_high = second.astype(BF16).astype(F32)
    second = jnp.concatenate([second_high, second - second_high, second_high], axis=1).astype(BF16)
    some = 4

    def pair_step(i, carry):
        reach = jnp.concatenate([dist[pl.ds(i * some + q, 1), :] for q in range(some)], axis=1)
        centres = 2.0 * lax.broadcasted_iota(jnp.int32, (16, some * KEYS), 0).astype(F32)
        away = reach - centres
        high, low = split(jnp.exp(away * away * -0.125))
        ones = jnp.ones((16, some * KEYS), BF16)
        half = 0.5 * tdot(first, jnp.concatenate([high, high, low, ones], axis=0))
        high, low = split(half + half * jnp.tanh(half))
        pair = jnp.dot(second, jnp.concatenate([high, high, low], axis=0), preferred_element_type=F32)
        for q in range(some):
            bias[pl.ds(pl.multiple_of((i * some + q) * HEADS, HEADS), HEADS), :] = pair[:, q * KEYS : (q + 1) * KEYS]
        return carry

    lax.fori_loop(0, ATOMS // some, pair_step, 0)

    ask.wait_recv()
    prepare(1)
    attend([(1, 0)])

    def relay_step(t, carry):
        near, far = 2 * t + 1, 2 * t + 2
        for part in range(2):
            hand(0, far, part, sibling).wait_recv()

            @pl.when((t < 2) | (part == 0))
            def _():
                hand(far, far + 2, part, along_z(2)).start()

            hand(0, RIGHT + far, part, sibling).wait_recv()

            @pl.when((t < 2) | (part == 1))
            def _():
                target = jnp.where(t < 2, RIGHT + far + 2, RIGHT)
                hand(RIGHT + far, target, part, along_z(-2)).start()

        for part in range(2):
            hand(far, far + 1, part, along_z(1)).start()
            hand(RIGHT + far, RIGHT + far + 1, part, along_z(-1)).start()
        have(near)
        have(RIGHT + near)
        attend([(q, k) for k in (far, RIGHT + far, near, RIGHT + near) for q in (0, 1)])
        return carry

    lax.fori_loop(0, 3, relay_step, 0)

    halo_copies[2].wait_recv()
    halo_copies[3].wait_recv()
    own_head = lax.broadcasted_iota(jnp.int32, (HEADS, WIDTH), 1) // HEAD == lax.broadcasted_iota(
        jnp.int32, (HEADS, WIDTH), 0
    )
    spread_q = jnp.where(own_head[None], own_q[...].astype(F32)[:, None, :], 0.0)
    spread_q = spread_q.reshape(ATOMS * HEADS, WIDTH).astype(BF16)
    near_keys = jnp.concatenate([near_kv[slot][:, :WIDTH] for slot in slots], axis=0)
    near_values = jnp.concatenate([near_kv[slot][:, WIDTH:] for slot in slots], axis=0)
    local = lax.dot_general(spread_q, near_keys, (((1,), (1,)), ((), ())), preferred_element_type=F32)
    local = local * HEAD**-0.5 + bias[...]
    local = jnp.where(live > 0, local, -1e30)
    weights = jnp.exp(local - jnp.max(local, axis=-1, keepdims=True))
    inverse = 1.0 / jnp.sum(weights, axis=-1, keepdims=True)
    mixed = jnp.dot(weights.astype(BF16), near_values, preferred_element_type=F32) * inverse
    mixed = jnp.where(own_head[None], mixed.reshape(ATOMS, HEADS, WIDTH), 0.0)
    local_out = jnp.sum(mixed, axis=1).astype(BF16).astype(F32)

    last = (RIGHT - 1, DEPTH - 1, RIGHT)
    for k in last:
        have(k)
    attend([(1, k) for k in last])
    head_rows = jnp.where(lax.broadcasted_iota(jnp.int32, (8, GROUP), 0) == 0, run_max[1], accum[1, 0:8, :])
    part_out[...] = jnp.concatenate([head_rows, accum[1, 16:48, :]], axis=0)
    give = remote(part_out, part_in, part_send, part_recv, sibling)
    give.start()
    attend([(0, k) for k in last])

    give.wait_recv()
    part = part_in[...]
    tops = [run_max[0], part[0:1]]
    sums = [accum[0, 6:7, :], part[6:7]]
    values = [accum[0, 16:48, :], part[8:40]]
    top = functools.reduce(jnp.maximum, tops)
    shares = [jnp.exp2(t - top) for t in tops]
    total = sum(share * one for share, one in zip(shares, sums))
    attended = sum(share * one for share, one in zip(shares, values)) / total

    attended = attended.astype(BF16).astype(F32).T.reshape(HEADS, 4, 8, HEAD)
    returning[...] = jnp.concatenate([attended[:, q] for q in range(4)], axis=-1)

    def back_copy(step):
        other, device = plane(step)
        return remote(
            returning.at[other],
            returned.at[head_here],
            back_send.at[step],
            back_recv.at[step],
            device,
        )

    def start_back(step, carry):
        back_copy(step).start()
        return carry

    lax.fori_loop(1, HEADS, start_back, 0)
    returned[head_here] = returning[head_here]

    def end_sends(step, carry):
        swap_copy(step).wait_send()
        for part in range(2):
            hand(0, step, part, sibling).wait_send()
        return carry

    lax.fori_loop(1, HEADS, end_sends, 0)
    ask.wait_send()
    give.wait_send()
    for k in range(len(moves)):
        pos_copy(k).wait_send()
    for copy in halo_copies:
        copy.wait_send()

    def end_back(step, carry):
        back_copy(step).wait_send()
        back_copy(step).wait_recv()
        return carry

    lax.fori_loop(1, HEADS, end_back, 0)
    global_out = jnp.concatenate(
        [
            jnp.concatenate([returned[head][:, q * HEAD : (q + 1) * HEAD] for head in range(HEADS)], axis=1)
            for q in range(4)
        ],
        axis=0,
    )
    combined = (local_out + global_out).astype(BF16)
    updated = floats + jnp.dot(combined, w_out[...], preferred_element_type=F32)
    out[...] = updated.astype(BF16)


def on_device(
    features,
    positions,
    cell_lengths,
    block_lists,
    image_offsets,
    block_valid,
    norm_gain,
    w_qkv,
    w_out,
    rbf_weight,
    rbf_offset,
    pair_weight,
    cosine_scale,
):
    hbm = pl.BlockSpec(memory_space=pltpu.HBM)
    dma = pltpu.SemaphoreType.DMA
    return pl.pallas_call(
        kernel,
        out_shape=jax.ShapeDtypeStruct((ATOMS, WIDTH), BF16),
        in_specs=[hbm] * 13,
        out_specs=pl.BlockSpec(memory_space=pltpu.VMEM),
        scratch_shapes=[
            pltpu.VMEM((ATOMS, WIDTH), BF16),
            pltpu.VMEM((3, ATOMS), F32),
            pltpu.SMEM((3,), F32),
            pltpu.SMEM((1, 8), jnp.int32),
            pltpu.SMEM((3, 1, 8), jnp.int32),
            pltpu.SMEM((1, 8), jnp.int32),
            pltpu.VMEM((1, WIDTH), F32),
            pltpu.VMEM((WIDTH, 3 * WIDTH), BF16),
            pltpu.VMEM((WIDTH, WIDTH), BF16),
            pltpu.VMEM((16, 64), F32),
            pltpu.VMEM((1, 64), F32),
            pltpu.VMEM((16, 64), F32),
            pltpu.SMEM((16,), F32),
            dma((13,)),
            pltpu.VMEM((9, ATOMS, 2 * WIDTH), BF16),
            pltpu.VMEM((9, 8, 128), F32),
            pltpu.VMEM((HEADS, ATOMS, 128), BF16),
            pltpu.VMEM((GROUP, 128), BF16),
            pltpu.VMEM((2, 48, GROUP), BF16),
            pltpu.VMEM((DEPTH, 80, GROUP), BF16),
            pltpu.VMEM((2, 96, GROUP), BF16),
            pltpu.VMEM((2, GROUP, GROUP), F32),
            pltpu.VMEM((2, 1, GROUP), F32),
            pltpu.VMEM((2, 48, GROUP), F32),
            pltpu.VMEM((40, GROUP), F32),
            pltpu.VMEM((40, GROUP), F32),
            pltpu.VMEM((ATOMS, KEYS), F32),
            pltpu.VMEM((ATOMS * HEADS, KEYS), F32),
            pltpu.VMEM((HEADS, 8, 128), F32),
            pltpu.VMEM((HEADS, 8, 128), F32),
            pltpu.VMEM((ATOMS, WIDTH), BF16),
            dma((8,)),
            dma((8,)),
            dma((4,)),
            dma((4,)),
            dma((16,)),
            dma((16,)),
            dma(()),
            dma(()),
            dma((2, 16)),
            dma((2, 16)),
            dma(()),
            dma(()),
            dma((16,)),
            dma((16,)),
        ],
        compiler_params=pltpu.CompilerParams(
            collective_id=0, has_side_effects=True, vmem_limit_bytes=63 * 2**20
        ),
    )(
        features,
        positions,
        cell_lengths,
        block_lists,
        image_offsets,
        block_valid,
        norm_gain.reshape(1, WIDTH),
        w_qkv,
        w_out,
        rbf_weight,
        rbf_offset.reshape(1, 64),
        pair_weight.T,
        cosine_scale,
    )


def solution(mesh):
    return jax.shard_map(
        on_device,
        mesh=mesh,
        in_specs=(
            P(("rows", "cols"), None),
            P(None, ("rows", "cols")),
            P(),
            P(("rows", "cols"), None),
            P(None, ("rows", "cols"), None),
            P(("rows", "cols"), None),
            P(),
            P(),
            P(),
            P(),
            P(),
            P(),
            P(),
        ),
        out_specs=P(("rows", "cols"), None),
        check_vma=False,
    )
```

```python
import functools
import math

import jax
import jax.numpy as jnp
from jax import lax
from jax.experimental import pallas as pl
from jax.experimental.pallas import tpu as pltpu
from jax.sharding import PartitionSpec as P

MESH = pl.DeviceIdType.MESH
F32 = jnp.float32
BF16 = jnp.bfloat16
LOG2E = math.log2(math.e)

ATOMS = 32
WIDTH = 512
HEADS = 16
HEAD = 32
GROUP = 512
KEYS = 256
ROWS = 16
COLS = 32
DEPTH = 16
RIGHT = 8


def tdot(a, b):
    return lax.dot_general(a, b, (((0,), (0,)), ((), ())), preferred_element_type=F32)


def split(value):
    high = value.astype(BF16)
    return high, (value - high.astype(F32)).astype(BF16)


def kernel(
    features_at,
    positions_at,
    lengths_at,
    lists_at,
    offsets_at,
    valid_at,
    gain_at,
    w_qkv_at,
    w_out_at,
    rbf_weight_at,
    rbf_offset_at,
    pair_weight_at,
    strengths_at,
    out,
    features,
    positions,
    lengths,
    lists,
    offsets,
    valid,
    gain,
    w_qkv,
    w_out,
    rbf_weight,
    rbf_offset,
    pair_weight,
    strengths,
    load_sem,
    near_kv,
    near_pos,
    pieces,
    gathered,
    asked,
    kv,
    queries,
    scores,
    run_max,
    accum,
    part_out,
    part_in,
    dist,
    bias,
    returning,
    returned,
    own_q,
    pos_send,
    pos_recv,
    halo_send,
    halo_recv,
    swap_send,
    swap_recv,
    ask_send,
    ask_recv,
    kv_send,
    kv_recv,
    part_send,
    part_recv,
    back_send,
    back_recv,
):
    row, col = lax.axis_index("rows"), lax.axis_index("cols")
    core = lax.rem(row, 2)
    x, y_lo = row // 4, lax.rem(row // 2, 2)
    y_hi, z = col // DEPTH, lax.rem(col, DEPTH)
    y = y_hi * 2 + y_lo

    head_here = x * 4 + y

    def plane(step):
        other = lax.rem(head_here + step, HEADS)
        oy = lax.rem(other, 4)
        return other, (other // 4 * 4 + lax.rem(oy, 2) * 2 + core, oy // 2 * DEPTH + z)

    def along_z(step):
        return (row, y_hi * DEPTH + lax.rem(z + step + DEPTH, DEPTH))

    sibling = (row + 1 - 2 * core, col)

    def beside(dr, dc):
        return (lax.rem(row + dr + ROWS, ROWS), lax.rem(col + dc + COLS, COLS))

    moves = [(dr, dc) for dr in (-1, 0, 1) for dc in (-1, 0, 1) if (dr, dc) != (0, 0)]

    def remote(src, dst, send, recv, device):
        return pltpu.make_async_remote_copy(
            src_ref=src, dst_ref=dst, send_sem=send, recv_sem=recv, device_id=device, device_id_type=MESH
        )

    loads = [
        pltpu.make_async_copy(src, dst, load_sem.at[i])
        for i, (src, dst) in enumerate(
            [
                (w_qkv_at, w_qkv),
                (features_at, features),
                (gain_at, gain),
                (positions_at, positions),
                (strengths_at, strengths),
                (lists_at, lists),
                (offsets_at, offsets),
                (lengths_at, lengths),
                (valid_at, valid),
                (rbf_weight_at, rbf_weight),
                (rbf_offset_at, rbf_offset),
                (pair_weight_at, pair_weight),
                (w_out_at, w_out),
            ]
        )
    ]
    for load in loads[:4]:
        load.start()

    barrier = pltpu.get_barrier_semaphore()

    def greet(device):
        pl.semaphore_signal(barrier, inc=1, device_id=device, device_id_type=MESH)

    def greet_plane(step, carry):
        greet(plane(step)[1])
        return carry

    lax.fori_loop(1, HEADS, greet_plane, 0)
    for step in (-2, -1, 1, 2):
        greet(along_z(step))
    for move in moves:
        greet(beside(*move))
    greet(sibling)
    for load in loads[4:]:
        load.start()

    for load in loads[:4]:
        load.wait()
    pos = positions[...]
    near_pos[4] = jnp.zeros((8, 128), F32)
    near_pos[4, 0:3, 0:ATOMS] = pos
    angles = (2.0 * math.pi) * pos
    waves = jnp.concatenate(
        [jnp.cos(angles), jnp.sin(angles), jnp.ones((1, ATOMS), F32), jnp.zeros((1, ATOMS), F32)], axis=0
    )
    wave_high = waves.astype(BF16).astype(F32)
    waves = jnp.concatenate([wave_high, waves - wave_high], axis=0).astype(BF16)
    place = lax.broadcasted_iota(jnp.int32, (16, 128), 0) + 96 == lax.broadcasted_iota(jnp.int32, (16, 128), 1)
    wave_lanes = tdot(waves, jnp.where(place, 1.0, 0.0).astype(BF16))[:, 96:128]

    floats = features[...].astype(F32)
    spread = jnp.mean(floats * floats, axis=-1, keepdims=True)
    normed = (floats * lax.rsqrt(spread + 1e-06) * gain[...]).astype(BF16)
    packed = jnp.dot(normed, w_qkv[...], preferred_element_type=F32)
    for head in range(HEADS):
        lo = head * HEAD
        pieces[head] = jnp.concatenate(
            [
                packed[:, lo : lo + HEAD],
                packed[:, WIDTH + lo : WIDTH + lo + HEAD],
                packed[:, 2 * WIDTH + lo : 2 * WIDTH + lo + HEAD],
                wave_lanes,
            ],
            axis=1,
        ).astype(BF16)
    own_q[...] = packed[:, :WIDTH].astype(BF16)
    near_kv[4] = packed[:, WIDTH:].astype(BF16)

    pl.semaphore_wait(barrier, HEADS - 1 + 4 + len(moves) + 1)

    def pos_copy(k):
        dr, dc = moves[k]
        return remote(
            near_pos.at[4],
            near_pos.at[(1 - dr) * 3 + (1 - dc)],
            pos_send.at[k],
            pos_recv.at[k],
            beside(dr, dc),
        )

    def swap_copy(step):
        other, device = plane(step)
        return remote(
            pieces.at[other],
            gathered.at[pl.ds(pl.multiple_of(head_here * ATOMS, ATOMS), ATOMS)],
            swap_send.at[step],
            swap_recv.at[step],
            device,
        )

    def start_swap(step, carry):
        swap_copy(step).start()
        return carry

    lax.fori_loop(1, HEADS, start_swap, 0)
    for k in range(len(moves)):
        pos_copy(k).start()
    gathered[pl.ds(pl.multiple_of(head_here * ATOMS, ATOMS), ATOMS), :] = pieces[head_here]

    halo_copies = [
        remote(near_kv.at[4], near_kv.at[3], halo_send.at[0], halo_recv.at[0], beside(0, 1)),
        remote(near_kv.at[4], near_kv.at[5], halo_send.at[1], halo_recv.at[1], beside(0, -1)),
        remote(near_kv.at[pl.ds(3, 3)], near_kv.at[pl.ds(0, 3)], halo_send.at[2], halo_recv.at[2], beside(1, 0)),
        remote(near_kv.at[pl.ds(3, 3)], near_kv.at[pl.ds(6, 3)], halo_send.at[3], halo_recv.at[3], beside(-1, 0)),
    ]
    halo_copies[0].start()
    halo_copies[1].start()

    for load in loads[4:]:
        load.wait()

    def end_swap(step, carry):
        swap_copy(step).wait_recv()
        return carry

    lax.fori_loop(1, HEADS, end_swap, 0)
    turned = gathered[...].astype(F32).T
    kv[0] = jnp.concatenate([turned[32:64], turned[96:112], turned[64:96]], axis=0).astype(BF16)
    asked[0] = jnp.concatenate([turned[0:32], turned[96:112]], axis=0).astype(BF16)

    def hand(source, target, part, device):
        rows = pl.ds(0, 48) if part == 0 else pl.ds(48, 32)
        return remote(
            kv.at[source, rows], kv.at[target, rows], kv_send.at[part, target], kv_recv.at[part, target], device
        )

    def have(target):
        for part in range(2):
            hand(0, target, part, sibling).wait_recv()

    for part in range(2):
        hand(0, 2, part, along_z(2)).start()
        hand(0, RIGHT + 2, part, along_z(-2)).start()
    ask = remote(asked.at[0], asked.at[1], ask_send, ask_recv, sibling)
    ask.start()
    for part in range(2):
        hand(0, 1, part, along_z(1)).start()
        hand(0, RIGHT + 1, part, along_z(-1)).start()

    def prepare(q):
        rows = asked[q].astype(F32)
        high, low = split(rows[0:32] * (HEAD**-0.5 * LOG2E))
        wave = rows[32:40] + rows[40:48]
        wave = jnp.where(lax.broadcasted_iota(jnp.int32, (8, GROUP), 0) < 6, wave, 0.0) * (strengths[head_here] * LOG2E)
        wave_high = wave.astype(BF16).astype(F32)
        zeros = jnp.zeros((8, GROUP), F32)
        queries[q] = jnp.concatenate(
            [
                high,
                jnp.concatenate([wave_high, wave_high], axis=0).astype(BF16),
                low,
                jnp.concatenate([wave - wave_high, zeros], axis=0).astype(BF16),
            ],
            axis=0,
        )

    run_max[...] = jnp.full(run_max.shape, -1e30, F32)
    accum[...] = jnp.zeros(accum.shape, F32)

    def put(slot, q, k):
        part = kv[k, 0:48, :]
        scores[slot] = tdot(jnp.concatenate([part, part], axis=0), queries[q])

    def soft(slot, q, k):
        value = scores[slot]
        old = run_max[q]
        new = jnp.maximum(old, jnp.max(value, axis=0, keepdims=True))
        weights = jnp.exp2(value - new).astype(BF16)
        added = jnp.dot(kv[k, 32:80, :], weights, preferred_element_type=F32)
        run_max[q] = new
        accum[q] = accum[q] * jnp.exp2(old - new) + added

    def attend(units, at=None, then=None):
        put(0, *units[0])
        for i, unit in enumerate(units):
            if i == at:
                then()
            if i + 1 < len(units):
                put((i + 1) % 2, *units[i + 1])
            soft(i % 2, *unit)

    prepare(0)
    attend([(0, 0)])
    halo_copies[0].wait_recv()
    halo_copies[1].wait_recv()
    halo_copies[2].start()
    halo_copies[3].start()

    for k in range(len(moves)):
        pos_copy(k).wait_recv()
    slots = []
    for e in range(8):
        block = lists[0, e]
        dr = lax.rem(block // COLS - row + 1 + ROWS, ROWS)
        dc = lax.rem(lax.rem(block, COLS) - col + 1 + COLS, COLS)
        slots.append(jnp.minimum(dr, 2) * 3 + jnp.minimum(dc, 2))
    key_pos = jnp.concatenate([near_pos[slot][:, 0:ATOMS] for slot in slots], axis=1)
    entry = lax.broadcasted_iota(jnp.int32, (1, KEYS), 1) // ATOMS
    own_pos = near_pos[4].T
    square = jnp.zeros((ATOMS, KEYS), F32)
    for c in range(3):
        shift = jnp.zeros((1, KEYS), F32)
        for e in range(8):
            shift = jnp.where(entry == e, offsets[c, 0, e].astype(F32), shift)
        step = (key_pos[c : c + 1, :] + shift - own_pos[0:ATOMS, c : c + 1]) * lengths[c]
        square = square + step * step
    dist[...] = jnp.sqrt(square + 0.25)
    live = jnp.zeros((1, KEYS), jnp.int32)
    for e in range(8):
        live = jnp.where(entry == e, valid[0, e], live)

    first_high, first_low = split(rbf_weight[...])
    shift_high = rbf_offset[...].astype(BF16).astype(F32)
    shift_rest = rbf_offset[...] - shift_high
    shift_mid = shift_rest.astype(BF16).astype(F32)
    which = lax.broadcasted_iota(jnp.int32, (16, 64), 0)
    shift_rows = jnp.where(
        which == 0, shift_high, jnp.where(which == 1, shift_mid, jnp.where(which == 2, shift_rest - shift_mid, 0.0))
    ).astype(BF16)
    first = jnp.concatenate([first_high, first_low, first_high, shift_rows], axis=0)
    second = pair_weight[...]
    second_high = second.astype(BF16).astype(F32)
    second = jnp.concatenate([second_high, second - second_high, second_high], axis=1).astype(BF16)
    some = 4

    def pair_step(i, carry):
        reach = jnp.concatenate([dist[pl.ds(i * some + q, 1), :] for q in range(some)], axis=1)
        centres = 2.0 * lax.broadcasted_iota(jnp.int32, (16, some * KEYS), 0).astype(F32)
        away = reach - centres
        high, low = split(jnp.exp(away * away * -0.125))
        ones = jnp.ones((16, some * KEYS), BF16)
        half = 0.5 * tdot(first, jnp.concatenate([high, high, low, ones], axis=0))
        high, low = split(half + half * jnp.tanh(half))
        pair = jnp.dot(second, jnp.concatenate([high, high, low], axis=0), preferred_element_type=F32)
        for q in range(some):
            bias[pl.ds(pl.multiple_of((i * some + q) * HEADS, HEADS), HEADS), :] = pair[:, q * KEYS : (q + 1) * KEYS]
        return carry

    lax.fori_loop(0, ATOMS // some, pair_step, 0)

    ask.wait_recv()
    prepare(1)
    attend([(1, 0)])

    def relay_step(t, carry):
        near, far = 2 * t + 1, 2 * t + 2
        for part in range(2):
            hand(0, far, part, sibling).wait_recv()

            @pl.when((t < 2) | (part == 0))
            def _():
                hand(far, far + 2, part, along_z(2)).start()

            hand(0, RIGHT + far, part, sibling).wait_recv()

            @pl.when((t < 2) | (part == 1))
            def _():
                target = jnp.where(t < 2, RIGHT + far + 2, RIGHT)
                hand(RIGHT + far, target, part, along_z(-2)).start()

        for part in range(2):
            hand(far, far + 1, part, along_z(1)).start()
            hand(RIGHT + far, RIGHT + far + 1, part, along_z(-1)).start()

        def nears():
            have(near)
            have(RIGHT + near)

        attend([(q, k) for k in (far, RIGHT + far, near, RIGHT + near) for q in (0, 1)], 3, nears)
        return carry

    lax.fori_loop(0, 3, relay_step, 0)

    halo_copies[2].wait_recv()
    halo_copies[3].wait_recv()
    own_head = lax.broadcasted_iota(jnp.int32, (HEADS, WIDTH), 1) // HEAD == lax.broadcasted_iota(
        jnp.int32, (HEADS, WIDTH), 0
    )
    spread_q = jnp.where(own_head[None], own_q[...].astype(F32)[:, None, :], 0.0)
    spread_q = spread_q.reshape(ATOMS * HEADS, WIDTH).astype(BF16)
    near_keys = jnp.concatenate([near_kv[slot][:, :WIDTH] for slot in slots], axis=0)
    near_values = jnp.concatenate([near_kv[slot][:, WIDTH:] for slot in slots], axis=0)
    local = lax.dot_general(spread_q, near_keys, (((1,), (1,)), ((), ())), preferred_element_type=F32)
    local = local * HEAD**-0.5 + bias[...]
    local = jnp.where(live > 0, local, -1e30)
    weights = jnp.exp(local - jnp.max(local, axis=-1, keepdims=True))
    inverse = 1.0 / jnp.sum(weights, axis=-1, keepdims=True)
    mixed = jnp.dot(weights.astype(BF16), near_values, preferred_element_type=F32) * inverse
    mixed = jnp.where(own_head[None], mixed.reshape(ATOMS, HEADS, WIDTH), 0.0)
    local_out = jnp.sum(mixed, axis=1).astype(BF16).astype(F32)

    last = (RIGHT, RIGHT - 1, DEPTH - 1)

    def last_nears():
        have(RIGHT - 1)
        have(DEPTH - 1)

    have(RIGHT)
    attend([(1, k) for k in last], 0, last_nears)
    head_rows = jnp.where(lax.broadcasted_iota(jnp.int32, (8, GROUP), 0) == 0, run_max[1], accum[1, 0:8, :])
    part_out[...] = jnp.concatenate([head_rows, accum[1, 16:48, :]], axis=0)
    give = remote(part_out, part_in, part_send, part_recv, sibling)
    give.start()
    attend([(0, k) for k in last])

    give.wait_recv()
    part = part_in[...]
    tops = [run_max[0], part[0:1]]
    sums = [accum[0, 6:7, :], part[6:7]]
    values = [accum[0, 16:48, :], part[8:40]]
    top = functools.reduce(jnp.maximum, tops)
    shares = [jnp.exp2(t - top) for t in tops]
    total = sum(share * one for share, one in zip(shares, sums))
    attended = sum(share * one for share, one in zip(shares, values)) / total

    attended = attended.astype(BF16).astype(F32).T.reshape(HEADS, 4, 8, HEAD)
    returning[...] = jnp.concatenate([attended[:, q] for q in range(4)], axis=-1)

    def back_copy(step):
        other, device = plane(step)
        return remote(
            returning.at[other],
            returned.at[head_here],
            back_send.at[step],
            back_recv.at[step],
            device,
        )

    def start_back(step, carry):
        back_copy(step).start()
        return carry

    lax.fori_loop(1, HEADS, start_back, 0)
    returned[head_here] = returning[head_here]

    def end_sends(step, carry):
        swap_copy(step).wait_send()
        for part in range(2):
            hand(0, step, part, sibling).wait_send()
        return carry

    lax.fori_loop(1, HEADS, end_sends, 0)
    ask.wait_send()
    give.wait_send()
    for k in range(len(moves)):
        pos_copy(k).wait_send()
    for copy in halo_copies:
        copy.wait_send()

    def end_back(step, carry):
        back_copy(step).wait_send()
        back_copy(step).wait_recv()
        return carry

    lax.fori_loop(1, HEADS, end_back, 0)
    global_out = jnp.concatenate(
        [
            jnp.concatenate([returned[head][:, q * HEAD : (q + 1) * HEAD] for head in range(HEADS)], axis=1)
            for q in range(4)
        ],
        axis=0,
    )
    combined = (local_out + global_out).astype(BF16)
    updated = floats + jnp.dot(combined, w_out[...], preferred_element_type=F32)
    out[...] = updated.astype(BF16)


def on_device(
    features,
    positions,
    cell_lengths,
    block_lists,
    image_offsets,
    block_valid,
    norm_gain,
    w_qkv,
    w_out,
    rbf_weight,
    rbf_offset,
    pair_weight,
    cosine_scale,
):
    hbm = pl.BlockSpec(memory_space=pltpu.HBM)
    dma = pltpu.SemaphoreType.DMA
    return pl.pallas_call(
        kernel,
        out_shape=jax.ShapeDtypeStruct((ATOMS, WIDTH), BF16),
        in_specs=[hbm] * 13,
        out_specs=pl.BlockSpec(memory_space=pltpu.VMEM),
        scratch_shapes=[
            pltpu.VMEM((ATOMS, WIDTH), BF16),
            pltpu.VMEM((3, ATOMS), F32),
            pltpu.SMEM((3,), F32),
            pltpu.SMEM((1, 8), jnp.int32),
            pltpu.SMEM((3, 1, 8), jnp.int32),
            pltpu.SMEM((1, 8), jnp.int32),
            pltpu.VMEM((1, WIDTH), F32),
            pltpu.VMEM((WIDTH, 3 * WIDTH), BF16),
            pltpu.VMEM((WIDTH, WIDTH), BF16),
            pltpu.VMEM((16, 64), F32),
            pltpu.VMEM((1, 64), F32),
            pltpu.VMEM((16, 64), F32),
            pltpu.SMEM((16,), F32),
            dma((13,)),
            pltpu.VMEM((9, ATOMS, 2 * WIDTH), BF16),
            pltpu.VMEM((9, 8, 128), F32),
            pltpu.VMEM((HEADS, ATOMS, 128), BF16),
            pltpu.VMEM((GROUP, 128), BF16),
            pltpu.VMEM((2, 48, GROUP), BF16),
            pltpu.VMEM((DEPTH, 80, GROUP), BF16),
            pltpu.VMEM((2, 96, GROUP), BF16),
            pltpu.VMEM((2, GROUP, GROUP), F32),
            pltpu.VMEM((2, 1, GROUP), F32),
            pltpu.VMEM((2, 48, GROUP), F32),
            pltpu.VMEM((40, GROUP), F32),
            pltpu.VMEM((40, GROUP), F32),
            pltpu.VMEM((ATOMS, KEYS), F32),
            pltpu.VMEM((ATOMS * HEADS, KEYS), F32),
            pltpu.VMEM((HEADS, 8, 128), F32),
            pltpu.VMEM((HEADS, 8, 128), F32),
            pltpu.VMEM((ATOMS, WIDTH), BF16),
            dma((8,)),
            dma((8,)),
            dma((4,)),
            dma((4,)),
            dma((16,)),
            dma((16,)),
            dma(()),
            dma(()),
            dma((2, 16)),
            dma((2, 16)),
            dma(()),
            dma(()),
            dma((16,)),
            dma((16,)),
        ],
        compiler_params=pltpu.CompilerParams(
            collective_id=0, has_side_effects=True, vmem_limit_bytes=63 * 2**20
        ),
    )(
        features,
        positions,
        cell_lengths,
        block_lists,
        image_offsets,
        block_valid,
        norm_gain.reshape(1, WIDTH),
        w_qkv,
        w_out,
        rbf_weight,
        rbf_offset.reshape(1, 64),
        pair_weight.T,
        cosine_scale,
    )


def solution(mesh):
    return jax.shard_map(
        on_device,
        mesh=mesh,
        in_specs=(
            P(("rows", "cols"), None),
            P(None, ("rows", "cols")),
            P(),
            P(("rows", "cols"), None),
            P(None, ("rows", "cols"), None),
            P(("rows", "cols"), None),
            P(),
            P(),
            P(),
            P(),
            P(),
            P(),
            P(),
        ),
        out_specs=P(("rows", "cols"), None),
        check_vma=False,
    )
```

```python
import functools
import math

import jax
import jax.numpy as jnp
from jax import lax
from jax.experimental import pallas as pl
from jax.experimental.pallas import tpu as pltpu
from jax.sharding import PartitionSpec as P

MESH = pl.DeviceIdType.MESH
F32 = jnp.float32
BF16 = jnp.bfloat16
LOG2E = math.log2(math.e)

ATOMS = 32
WIDTH = 512
HEADS = 16
HEAD = 32
GROUP = 512
KEYS = 256
ROWS = 16
COLS = 32
DEPTH = 16
RIGHT = 8


def tdot(a, b):
    return lax.dot_general(a, b, (((0,), (0,)), ((), ())), preferred_element_type=F32)


def split(value):
    high = value.astype(BF16)
    return high, (value - high.astype(F32)).astype(BF16)


def kernel(
    features_at,
    positions_at,
    lengths_at,
    lists_at,
    offsets_at,
    valid_at,
    gain_at,
    w_qkv_at,
    w_out_at,
    rbf_weight_at,
    rbf_offset_at,
    pair_weight_at,
    strengths_at,
    out,
    features,
    positions,
    lengths,
    lists,
    offsets,
    valid,
    gain,
    w_qkv,
    w_out,
    rbf_weight,
    rbf_offset,
    pair_weight,
    strengths,
    load_sem,
    near_kv,
    near_pos,
    pieces,
    gathered,
    asked,
    kv,
    queries,
    scores,
    run_max,
    accum,
    part_out,
    part_in,
    dist,
    bias,
    returning,
    returned,
    own_q,
    pos_send,
    pos_recv,
    halo_send,
    halo_recv,
    swap_send,
    swap_recv,
    ask_send,
    ask_recv,
    kv_send,
    kv_recv,
    part_send,
    part_recv,
    back_send,
    back_recv,
):
    row, col = lax.axis_index("rows"), lax.axis_index("cols")
    core = lax.rem(row, 2)
    x, y_lo = row // 4, lax.rem(row // 2, 2)
    y_hi, z = col // DEPTH, lax.rem(col, DEPTH)
    y = y_hi * 2 + y_lo

    head_here = x * 4 + y

    def plane(step):
        other = lax.rem(head_here + step, HEADS)
        oy = lax.rem(other, 4)
        return other, (other // 4 * 4 + lax.rem(oy, 2) * 2 + core, oy // 2 * DEPTH + z)

    def along_z(step):
        return (row, y_hi * DEPTH + lax.rem(z + step + DEPTH, DEPTH))

    sibling = (row + 1 - 2 * core, col)

    def beside(dr, dc):
        return (lax.rem(row + dr + ROWS, ROWS), lax.rem(col + dc + COLS, COLS))

    moves = [(dr, dc) for dr in (-1, 0, 1) for dc in (-1, 0, 1) if (dr, dc) != (0, 0)]

    def remote(src, dst, send, recv, device):
        return pltpu.make_async_remote_copy(
            src_ref=src, dst_ref=dst, send_sem=send, recv_sem=recv, device_id=device, device_id_type=MESH
        )

    loads = [
        pltpu.make_async_copy(src, dst, load_sem.at[i])
        for i, (src, dst) in enumerate(
            [
                (w_qkv_at, w_qkv),
                (features_at, features),
                (gain_at, gain),
                (positions_at, positions),
                (strengths_at, strengths),
                (lists_at, lists),
                (offsets_at, offsets),
                (lengths_at, lengths),
                (valid_at, valid),
                (rbf_weight_at, rbf_weight),
                (rbf_offset_at, rbf_offset),
                (pair_weight_at, pair_weight),
                (w_out_at, w_out),
            ]
        )
    ]
    for load in loads[:4]:
        load.start()

    barrier = pltpu.get_barrier_semaphore()

    def greet(device):
        pl.semaphore_signal(barrier, inc=1, device_id=device, device_id_type=MESH)

    def greet_plane(step, carry):
        greet(plane(step)[1])
        return carry

    for step in range(1, HEADS):
        greet_plane(step, 0)
    for step in (-2, -1, 1, 2):
        greet(along_z(step))
    for move in moves:
        greet(beside(*move))
    greet(sibling)
    for load in loads[4:]:
        load.start()

    for load in loads[:4]:
        load.wait()
    pos = positions[...]
    near_pos[4] = jnp.zeros((8, 128), F32)
    near_pos[4, 0:3, 0:ATOMS] = pos
    angles = (2.0 * math.pi) * pos
    waves = jnp.concatenate(
        [jnp.cos(angles), jnp.sin(angles), jnp.ones((1, ATOMS), F32), jnp.zeros((1, ATOMS), F32)], axis=0
    )
    wave_high = waves.astype(BF16).astype(F32)
    waves = jnp.concatenate([wave_high, waves - wave_high], axis=0).astype(BF16)
    place = lax.broadcasted_iota(jnp.int32, (16, 128), 0) + 96 == lax.broadcasted_iota(jnp.int32, (16, 128), 1)
    wave_lanes = tdot(waves, jnp.where(place, 1.0, 0.0).astype(BF16))[:, 96:128]

    floats = features[...].astype(F32)
    spread = jnp.mean(floats * floats, axis=-1, keepdims=True)
    normed = (floats * lax.rsqrt(spread + 1e-06) * gain[...]).astype(BF16)
    packed = jnp.dot(normed, w_qkv[...], preferred_element_type=F32)
    for head in range(HEADS):
        lo = head * HEAD
        pieces[head] = jnp.concatenate(
            [
                packed[:, lo : lo + HEAD],
                packed[:, WIDTH + lo : WIDTH + lo + HEAD],
                packed[:, 2 * WIDTH + lo : 2 * WIDTH + lo + HEAD],
                wave_lanes,
            ],
            axis=1,
        ).astype(BF16)
    own_q[...] = packed[:, :WIDTH].astype(BF16)
    near_kv[4] = packed[:, WIDTH:].astype(BF16)

    pl.semaphore_wait(barrier, HEADS - 1 + 4 + len(moves) + 1)

    def pos_copy(k):
        dr, dc = moves[k]
        return remote(
            near_pos.at[4],
            near_pos.at[(1 - dr) * 3 + (1 - dc)],
            pos_send.at[k],
            pos_recv.at[k],
            beside(dr, dc),
        )

    def swap_copy(step):
        other, device = plane(step)
        return remote(
            pieces.at[other],
            gathered.at[pl.ds(pl.multiple_of(head_here * ATOMS, ATOMS), ATOMS)],
            swap_send.at[step],
            swap_recv.at[step],
            device,
        )

    def start_swap(step, carry):
        swap_copy(step).start()
        return carry

    for step in range(1, HEADS):
        start_swap(step, 0)
    for k in range(len(moves)):
        pos_copy(k).start()
    gathered[pl.ds(pl.multiple_of(head_here * ATOMS, ATOMS), ATOMS), :] = pieces[head_here]

    halo_copies = [
        remote(near_kv.at[4], near_kv.at[3], halo_send.at[0], halo_recv.at[0], beside(0, 1)),
        remote(near_kv.at[4], near_kv.at[5], halo_send.at[1], halo_recv.at[1], beside(0, -1)),
        remote(near_kv.at[pl.ds(3, 3)], near_kv.at[pl.ds(0, 3)], halo_send.at[2], halo_recv.at[2], beside(1, 0)),
        remote(near_kv.at[pl.ds(3, 3)], near_kv.at[pl.ds(6, 3)], halo_send.at[3], halo_recv.at[3], beside(-1, 0)),
    ]
    halo_copies[0].start()
    halo_copies[1].start()

    for load in loads[4:]:
        load.wait()

    def end_swap(step, carry):
        swap_copy(step).wait_recv()
        return carry

    lax.fori_loop(1, HEADS, end_swap, 0)
    turned = gathered[...].astype(F32).T
    kv[0] = jnp.concatenate([turned[32:64], turned[96:112], turned[64:96]], axis=0).astype(BF16)
    asked[0] = jnp.concatenate([turned[0:32], turned[96:112]], axis=0).astype(BF16)

    def hand(source, target, part, device):
        rows = pl.ds(0, 48) if part == 0 else pl.ds(48, 32)
        return remote(
            kv.at[source, rows], kv.at[target, rows], kv_send.at[part, target], kv_recv.at[part, target], device
        )

    def have(target):
        for part in range(2):
            hand(0, target, part, sibling).wait_recv()

    for part in range(2):
        hand(0, 2, part, along_z(2)).start()
        hand(0, RIGHT + 2, part, along_z(-2)).start()
    ask = remote(asked.at[0], asked.at[1], ask_send, ask_recv, sibling)
    ask.start()
    for part in range(2):
        hand(0, 1, part, along_z(1)).start()
        hand(0, RIGHT + 1, part, along_z(-1)).start()

    def prepare(q):
        rows = asked[q].astype(F32)
        high, low = split(rows[0:32] * (HEAD**-0.5 * LOG2E))
        wave = rows[32:40] + rows[40:48]
        wave = jnp.where(lax.broadcasted_iota(jnp.int32, (8, GROUP), 0) < 6, wave, 0.0) * (strengths[head_here] * LOG2E)
        wave_high = wave.astype(BF16).astype(F32)
        zeros = jnp.zeros((8, GROUP), F32)
        queries[q] = jnp.concatenate(
            [
                high,
                jnp.concatenate([wave_high, wave_high], axis=0).astype(BF16),
                low,
                jnp.concatenate([wave - wave_high, zeros], axis=0).astype(BF16),
            ],
            axis=0,
        )

    run_max[...] = jnp.full(run_max.shape, -1e30, F32)
    accum[...] = jnp.zeros(accum.shape, F32)

    def put(slot, q, k):
        part = kv[k, 0:48, :]
        scores[slot] = tdot(jnp.concatenate([part, part], axis=0), queries[q])

    def soft(slot, q, k):
        value = scores[slot]
        old = run_max[q]
        new = jnp.maximum(old, jnp.max(value, axis=0, keepdims=True))
        weights = jnp.exp2(value - new).astype(BF16)
        added = jnp.dot(kv[k, 32:80, :], weights, preferred_element_type=F32)
        run_max[q] = new
        accum[q] = accum[q] * jnp.exp2(old - new) + added

    def attend(units, at=None, then=None):
        put(0, *units[0])
        for i, unit in enumerate(units):
            if i == at:
                then()
            if i + 1 < len(units):
                put((i + 1) % 2, *units[i + 1])
            soft(i % 2, *unit)

    prepare(0)
    attend([(0, 0)])
    halo_copies[0].wait_recv()
    halo_copies[1].wait_recv()
    halo_copies[2].start()
    halo_copies[3].start()

    for k in range(len(moves)):
        pos_copy(k).wait_recv()
    slots = []
    for e in range(8):
        block = lists[0, e]
        dr = lax.rem(block // COLS - row + 1 + ROWS, ROWS)
        dc = lax.rem(lax.rem(block, COLS) - col + 1 + COLS, COLS)
        slots.append(jnp.minimum(dr, 2) * 3 + jnp.minimum(dc, 2))
    key_pos = jnp.concatenate([near_pos[slot][:, 0:ATOMS] for slot in slots], axis=1)
    entry = lax.broadcasted_iota(jnp.int32, (1, KEYS), 1) // ATOMS
    own_pos = near_pos[4].T
    square = jnp.zeros((ATOMS, KEYS), F32)
    for c in range(3):
        shift = jnp.zeros((1, KEYS), F32)
        for e in range(8):
            shift = jnp.where(entry == e, offsets[c, 0, e].astype(F32), shift)
        step = (key_pos[c : c + 1, :] + shift - own_pos[0:ATOMS, c : c + 1]) * lengths[c]
        square = square + step * step
    dist[...] = jnp.sqrt(square + 0.25)
    live = jnp.zeros((1, KEYS), jnp.int32)
    for e in range(8):
        live = jnp.where(entry == e, valid[0, e], live)

    first_high, first_low = split(rbf_weight[...])
    shift_high = rbf_offset[...].astype(BF16).astype(F32)
    shift_rest = rbf_offset[...] - shift_high
    shift_mid = shift_rest.astype(BF16).astype(F32)
    which = lax.broadcasted_iota(jnp.int32, (16, 64), 0)
    shift_rows = jnp.where(
        which == 0, shift_high, jnp.where(which == 1, shift_mid, jnp.where(which == 2, shift_rest - shift_mid, 0.0))
    ).astype(BF16)
    first = jnp.concatenate([first_high, first_low, first_high, shift_rows], axis=0)
    second = pair_weight[...]
    second_high = second.astype(BF16).astype(F32)
    second = jnp.concatenate([second_high, second - second_high, second_high], axis=1).astype(BF16)
    some = 4

    def pair_step(i, carry):
        reach = jnp.concatenate([dist[pl.ds(i * some + q, 1), :] for q in range(some)], axis=1)
        centres = 2.0 * lax.broadcasted_iota(jnp.int32, (16, some * KEYS), 0).astype(F32)
        away = reach - centres
        high, low = split(jnp.exp(away * away * -0.125))
        ones = jnp.ones((16, some * KEYS), BF16)
        half = 0.5 * tdot(first, jnp.concatenate([high, high, low, ones], axis=0))
        high, low = split(half + half * jnp.tanh(half))
        pair = jnp.dot(second, jnp.concatenate([high, high, low], axis=0), preferred_element_type=F32)
        for q in range(some):
            bias[pl.ds(pl.multiple_of((i * some + q) * HEADS, HEADS), HEADS), :] = pair[:, q * KEYS : (q + 1) * KEYS]
        return carry

    lax.fori_loop(0, ATOMS // some, pair_step, 0)

    ask.wait_recv()
    prepare(1)
    attend([(1, 0)])

    def relay_step(t, carry):
        near, far = 2 * t + 1, 2 * t + 2
        for part in range(2):
            hand(0, far, part, sibling).wait_recv()

            @pl.when((t < 2) | (part == 0))
            def _():
                hand(far, far + 2, part, along_z(2)).start()

            hand(0, RIGHT + far, part, sibling).wait_recv()

            @pl.when((t < 2) | (part == 1))
            def _():
                target = jnp.where(t < 2, RIGHT + far + 2, RIGHT)
                hand(RIGHT + far, target, part, along_z(-2)).start()

        for part in range(2):
            hand(far, far + 1, part, along_z(1)).start()
            hand(RIGHT + far, RIGHT + far + 1, part, along_z(-1)).start()

        def nears():
            have(near)
            have(RIGHT + near)

        attend([(q, k) for k in (far, RIGHT + far, near, RIGHT + near) for q in (0, 1)], 3, nears)
        return carry

    lax.fori_loop(0, 3, relay_step, 0)

    halo_copies[2].wait_recv()
    halo_copies[3].wait_recv()
    own_head = lax.broadcasted_iota(jnp.int32, (HEADS, WIDTH), 1) // HEAD == lax.broadcasted_iota(
        jnp.int32, (HEADS, WIDTH), 0
    )
    spread_q = jnp.where(own_head[None], own_q[...].astype(F32)[:, None, :], 0.0)
    spread_q = spread_q.reshape(ATOMS * HEADS, WIDTH).astype(BF16)
    near_keys = jnp.concatenate([near_kv[slot][:, :WIDTH] for slot in slots], axis=0)
    near_values = jnp.concatenate([near_kv[slot][:, WIDTH:] for slot in slots], axis=0)
    local = lax.dot_general(spread_q, near_keys, (((1,), (1,)), ((), ())), preferred_element_type=F32)
    local = local * HEAD**-0.5 + bias[...]
    local = jnp.where(live > 0, local, -1e30)
    weights = jnp.exp(local - jnp.max(local, axis=-1, keepdims=True))
    inverse = 1.0 / jnp.sum(weights, axis=-1, keepdims=True)
    mixed = jnp.dot(weights.astype(BF16), near_values, preferred_element_type=F32) * inverse
    mixed = jnp.where(own_head[None], mixed.reshape(ATOMS, HEADS, WIDTH), 0.0)
    local_out = jnp.sum(mixed, axis=1).astype(BF16).astype(F32)

    last = (RIGHT, RIGHT - 1, DEPTH - 1)

    def last_nears():
        have(RIGHT - 1)
        have(DEPTH - 1)

    have(RIGHT)
    attend([(1, k) for k in last], 0, last_nears)
    head_rows = jnp.where(lax.broadcasted_iota(jnp.int32, (8, GROUP), 0) == 0, run_max[1], accum[1, 0:8, :])
    part_out[...] = jnp.concatenate([head_rows, accum[1, 16:48, :]], axis=0)
    give = remote(part_out, part_in, part_send, part_recv, sibling)
    give.start()
    attend([(0, k) for k in last])

    give.wait_recv()
    part = part_in[...]
    tops = [run_max[0], part[0:1]]
    sums = [accum[0, 6:7, :], part[6:7]]
    values = [accum[0, 16:48, :], part[8:40]]
    top = functools.reduce(jnp.maximum, tops)
    shares = [jnp.exp2(t - top) for t in tops]
    total = sum(share * one for share, one in zip(shares, sums))
    attended = sum(share * one for share, one in zip(shares, values)) / total

    attended = attended.astype(BF16).astype(F32).T.reshape(HEADS, 4, 8, HEAD)
    returning[...] = jnp.concatenate([attended[:, q] for q in range(4)], axis=-1)

    def back_copy(step):
        other, device = plane(step)
        return remote(
            returning.at[other],
            returned.at[head_here],
            back_send.at[step],
            back_recv.at[step],
            device,
        )

    def start_back(step, carry):
        back_copy(step).start()
        return carry

    for step in range(1, HEADS):
        start_back(step, 0)
    returned[head_here] = returning[head_here]

    def end_sends(step, carry):
        swap_copy(step).wait_send()
        for part in range(2):
            hand(0, step, part, sibling).wait_send()
        return carry

    lax.fori_loop(1, HEADS, end_sends, 0)
    ask.wait_send()
    give.wait_send()
    for k in range(len(moves)):
        pos_copy(k).wait_send()
    for copy in halo_copies:
        copy.wait_send()

    def end_back(step, carry):
        back_copy(step).wait_send()
        back_copy(step).wait_recv()
        return carry

    lax.fori_loop(1, HEADS, end_back, 0)
    global_out = jnp.concatenate(
        [
            jnp.concatenate([returned[head][:, q * HEAD : (q + 1) * HEAD] for head in range(HEADS)], axis=1)
            for q in range(4)
        ],
        axis=0,
    )
    combined = (local_out + global_out).astype(BF16)
    updated = floats + jnp.dot(combined, w_out[...], preferred_element_type=F32)
    out[...] = updated.astype(BF16)


def on_device(
    features,
    positions,
    cell_lengths,
    block_lists,
    image_offsets,
    block_valid,
    norm_gain,
    w_qkv,
    w_out,
    rbf_weight,
    rbf_offset,
    pair_weight,
    cosine_scale,
):
    hbm = pl.BlockSpec(memory_space=pltpu.HBM)
    dma = pltpu.SemaphoreType.DMA
    return pl.pallas_call(
        kernel,
        out_shape=jax.ShapeDtypeStruct((ATOMS, WIDTH), BF16),
        in_specs=[hbm] * 13,
        out_specs=pl.BlockSpec(memory_space=pltpu.VMEM),
        scratch_shapes=[
            pltpu.VMEM((ATOMS, WIDTH), BF16),
            pltpu.VMEM((3, ATOMS), F32),
            pltpu.SMEM((3,), F32),
            pltpu.SMEM((1, 8), jnp.int32),
            pltpu.SMEM((3, 1, 8), jnp.int32),
            pltpu.SMEM((1, 8), jnp.int32),
            pltpu.VMEM((1, WIDTH), F32),
            pltpu.VMEM((WIDTH, 3 * WIDTH), BF16),
            pltpu.VMEM((WIDTH, WIDTH), BF16),
            pltpu.VMEM((16, 64), F32),
            pltpu.VMEM((1, 64), F32),
            pltpu.VMEM((16, 64), F32),
            pltpu.SMEM((16,), F32),
            dma((13,)),
            pltpu.VMEM((9, ATOMS, 2 * WIDTH), BF16),
            pltpu.VMEM((9, 8, 128), F32),
            pltpu.VMEM((HEADS, ATOMS, 128), BF16),
            pltpu.VMEM((GROUP, 128), BF16),
            pltpu.VMEM((2, 48, GROUP), BF16),
            pltpu.VMEM((DEPTH, 80, GROUP), BF16),
            pltpu.VMEM((2, 96, GROUP), BF16),
            pltpu.VMEM((2, GROUP, GROUP), F32),
            pltpu.VMEM((2, 1, GROUP), F32),
            pltpu.VMEM((2, 48, GROUP), F32),
            pltpu.VMEM((40, GROUP), F32),
            pltpu.VMEM((40, GROUP), F32),
            pltpu.VMEM((ATOMS, KEYS), F32),
            pltpu.VMEM((ATOMS * HEADS, KEYS), F32),
            pltpu.VMEM((HEADS, 8, 128), F32),
            pltpu.VMEM((HEADS, 8, 128), F32),
            pltpu.VMEM((ATOMS, WIDTH), BF16),
            dma((8,)),
            dma((8,)),
            dma((4,)),
            dma((4,)),
            dma((16,)),
            dma((16,)),
            dma(()),
            dma(()),
            dma((2, 16)),
            dma((2, 16)),
            dma(()),
            dma(()),
            dma((16,)),
            dma((16,)),
        ],
        compiler_params=pltpu.CompilerParams(
            collective_id=0, has_side_effects=True, vmem_limit_bytes=63 * 2**20
        ),
    )(
        features,
        positions,
        cell_lengths,
        block_lists,
        image_offsets,
        block_valid,
        norm_gain.reshape(1, WIDTH),
        w_qkv,
        w_out,
        rbf_weight,
        rbf_offset.reshape(1, 64),
        pair_weight.T,
        cosine_scale,
    )


def solution(mesh):
    return jax.shard_map(
        on_device,
        mesh=mesh,
        in_specs=(
            P(("rows", "cols"), None),
            P(None, ("rows", "cols")),
            P(),
            P(("rows", "cols"), None),
            P(None, ("rows", "cols"), None),
            P(("rows", "cols"), None),
            P(),
            P(),
            P(),
            P(),
            P(),
            P(),
            P(),
        ),
        out_specs=P(("rows", "cols"), None),
        check_vma=False,
    )
```
